256 devices in a mesh: ctx: 32 (over y, z), tp: 8 (over x, core).
Axes of the slice: x: 4, y: 4, z: 8, core: 2. Of those that a mesh axis runs over, the one named last changes fastest.
Arguments:
- hidden_in: bfloat16 [4096, 5120], P('ctx', 'tp'), may hold values from -60 to 60
- norm_gain: bfloat16 [5120], P('tp'), may hold values from 0.099609375 to 1.8984375
- out_grad: bfloat16 [4096, 5120], P('ctx', 'tp'), may hold values from -6 to 6
- router_score: bfloat16 [4096], P('ctx'), may hold values from 0.19921875 to 1.5
- expert_ids: int32 [4096, 1], P('ctx'), may hold values from 0 to 7; in each aligned block of 128 rows (0 to 127, 128 to 255, ...) at most 24 rows name the same one
- gate_saved: bfloat16 [32, 2048, 768], P('ctx', 'tp'), may hold values from -6 to 6
- up_saved: bfloat16 [32, 2048, 768], P('ctx', 'tp'), may hold values from -6 to 6
- w_gate: bfloat16 [32, 5120, 2048], P('ctx', 'tp'), may hold values from -0.078125 to 0.078125
- w_up: bfloat16 [32, 5120, 2048], P('ctx', 'tp'), may hold values from -0.078125 to 0.078125
- w_down: bfloat16 [32, 2048, 5120], P('ctx', None, 'tp'), may hold values from -0.0625 to 0.0625
- w_out: bfloat16 [5120, 5120], P('tp', 'ctx'), may hold values from -0.078125 to 0.078125
- queries: bfloat16 [4096, 5120], P('ctx', 'tp'), may hold values from -18 to 18
- keys: bfloat16 [4096, 1024], P('ctx', 'tp'), may hold values from -18 to 18
- values: bfloat16 [4096, 1024], P('ctx', 'tp'), may hold values from -6 to 6
Outputs:
- d_hidden: bfloat16 [4096, 5120], P('ctx', 'tp')
- router_grad: float32 [4096], P('ctx')
- query_grad: bfloat16 [4096, 5120], P('ctx', 'tp')
- key_grad: bfloat16 [4096, 1024], P('ctx', 'tp')
- value_grad: bfloat16 [4096, 1024], P('ctx', 'tp')
The draws below stay inside these ranges and needn't reach their ends.
Inputs may be any that keep to these rules, and one draw needn't show every extreme that they name: `expert_ids`: in the 128 tokens of one device no expert is named more than 24 times.
All inputs are finite; a program needn't handle non-finite values.
Results may differ from the reference program's by a relative error of at most 0.035.
Values may be sent and summed in bfloat16 or wider, within the bound.
A program may use at most 128 MiB of HBM per device.

```python
import math
import jax
import jax.numpy as jnp
import numpy as np
from jax import lax

D = 5120
FF = 8192
QH = 40
KVH = 8
HD = 128
EXPERTS = 8
TOK_DEV = 128
CAP = 24
TOKENS = 4096
GROUP = 4
FF_GRP = 2048
SLOTS = 768
N_CTX = 32
N_TP = 8


def draw_queries(key, part):
    key = jax.random.fold_in(key, 11)
    return jnp.clip(jax.random.normal(key, (TOKENS, QH * HD), jnp.float32), -6.0, 6.0).astype(jnp.bfloat16)


def draw_keys(key, part):
    key = jax.random.fold_in(key, 12)
    return jnp.clip(jax.random.normal(key, (TOKENS, KVH * HD), jnp.float32), -6.0, 6.0).astype(jnp.bfloat16)


def draw_hidden_in(key, part):
    key = jax.random.fold_in(key, 13)
    column_scale = jnp.exp(1.0986123 * jnp.arange(D, dtype=jnp.float32)[None, :] / (D - 1))
    return (jnp.clip(jax.random.normal(key, (TOKENS, D), jnp.float32), -6.0, 6.0) * column_scale).astype(jnp.bfloat16)


def shard_levels(own_key, dims, cuts, smallest, largest):
    gain, own = 1.0, jax.random.fold_in(own_key, 6)
    for position, shards_of in cuts:
        draws = jnp.exp(jax.random.uniform(jax.random.fold_in(own, position), (shards_of,), jnp.float32, smallest / len(cuts), largest / len(cuts)))
        gain = gain * jnp.repeat(draws, dims[position] // shards_of).reshape([-1 if axis == position else 1 for axis in range(len(dims))])
    return gain


def assign_block(own_key, own, number, rows, count, top, reach, skew):
    sequence = jax.random.permutation(own_key, count)
    packed, common = load_shares(count, rows * top, reach, skew, True), load_shares(count, rows * top, reach, skew, False)
    places = jnp.arange(count)

    def named(sizes, turn):
        used = int((sizes > 0).sum())
        fixed = max(1, used // 4)
        moved = fixed + (places - fixed + turn * (used - fixed)) % max(1, count - fixed)
        return jnp.zeros((count,), jnp.int32).at[sequence[jnp.where(places < fixed, places, moved)]].set(jnp.asarray(sizes, jnp.int32))

    sizes = jnp.where(number % 4 == 0, named(packed, number // 4), named(common, number - number // 4 - 1))
    mixed = jax.random.permutation(jax.random.fold_in(own, 3), count)
    donor, sink = mixed[0:count // 2 * 2:2], mixed[1:count // 2 * 2:2]
    room = jnp.minimum(sizes[donor] - 1, reach - sizes[sink]) // 2
    room = jnp.where((donor == sequence[0]) | (sink == sequence[0]) | (sizes[sink] == 0), 0, jnp.maximum(room, 0))
    moved = jax.random.randint(jax.random.fold_in(own, 4), (count // 2,), 0, 1 << 20) % (room + 1)
    sizes = sizes.at[donor].add(-moved).at[sink].add(moved)
    items = jnp.searchsorted(jnp.cumsum(sizes), jnp.arange(rows * top), side="right").astype(jnp.int32)
    table = items.reshape(top, rows).T
    table = table[jax.random.permutation(jax.random.fold_in(own, 1), rows)]
    turn = jax.random.randint(jax.random.fold_in(own, 2), (rows, 1), 0, top)
    return jnp.take_along_axis(table, (jnp.arange(top)[None, :] + turn) % top, axis=1)


def load_shares(number_of, total, most, lean, full):
    loads = [(1 << 20) // math.isqrt(standing ** lean) + 1 for standing in range(1, number_of + 1)]
    largest = most if full else min(most, max(-(-total // number_of), total * loads[0] // sum(loads)))
    least = 1 if total - largest >= number_of - 1 else 0
    counts, rest = [largest] + [least] * (number_of - 1), total - largest - least * (number_of - 1)
    while rest > 0:
        candidates = [i for i in range(1, number_of) if counts[i] < largest] or [i for i in range(1, number_of) if counts[i] < most]
        whole, budget = sum([loads[i] for i in candidates]), rest
        for i in candidates:
            extra = min(most - counts[i], max(1, budget * loads[i] // whole), rest)
            counts[i] = counts[i] + extra
            rest = rest - extra
    return np.array(counts)


def noise(stream_key, shape, scale, most, cuts=(), held_as=jnp.bfloat16):
    gain = shard_levels(stream_key, shape, cuts, -0.22, 0.18) if cuts else 1.0
    values = jax.random.normal(stream_key, shape, jnp.float32) * scale * gain
    return jnp.minimum(jnp.maximum(values, -most), most).astype(held_as)


def setup_inputs(seed: int = 0) -> dict:
    streams_of = jax.random.split(jax.random.key(seed), 15)
    hidden_in = draw_hidden_in(jax.random.fold_in(streams_of[14], 71), 0)
    norm_gain = jnp.clip(1.0 + 0.18 * jax.random.normal(streams_of[1], (D,), jnp.float32), 0.099609375, 1.8984375).astype(jnp.bfloat16)
    out_grad = noise(streams_of[2], (TOKENS, D), 1.0, 6.0, ((0, 32), (1, 8)))
    router_score = jnp.clip(0.19921875 + 1.3007812 * jax.random.uniform(streams_of[3], (TOKENS,), jnp.float32) ** shard_levels(streams_of[3], (TOKENS,), ((0, 32),), -0.2, 0.2), 0.19921875, 1.5).astype(jnp.bfloat16)
    expert_ids_keys = jax.random.split(jax.random.fold_in(streams_of[4], 1), TOKENS // TOK_DEV)
    expert_ids_turns = jax.random.permutation(jax.random.fold_in(streams_of[4], 3), TOKENS // TOK_DEV)
    expert_ids = jax.vmap(lambda own, number: assign_block(jax.random.fold_in(streams_of[4], 2), own, number, TOK_DEV, EXPERTS, 1, CAP, 2))(expert_ids_keys, expert_ids_turns).reshape((TOKENS, 1))
    gate_saved = noise(streams_of[5], (N_CTX, FF_GRP, SLOTS), 1.0, 6.0, ((0, 32), (1, 8)))
    up_saved = noise(streams_of[6], (N_CTX, FF_GRP, SLOTS), 1.0, 6.0, ((0, 32), (1, 8)))
    w_gate = noise(streams_of[7], (N_CTX, D, FF_GRP), D ** -0.5, 0.078125, ((0, 32), (1, 8)))
    w_up = noise(streams_of[8], (N_CTX, D, FF_GRP), D ** -0.5, 0.078125, ((0, 32), (1, 8)))
    w_down = noise(streams_of[9], (N_CTX, FF_GRP, D), FF ** -0.5, 0.0625, ((0, 32), (2, 8)))
    w_out = noise(streams_of[10], (QH * HD, D), (QH * HD) ** -0.5, 0.078125, ((0, 8), (1, 32)))
    queries = draw_queries(jax.random.fold_in(streams_of[14], 71), 0)
    keys = draw_keys(jax.random.fold_in(streams_of[14], 71), 0)
    values = noise(streams_of[13], (TOKENS, KVH * HD), 1.0, 6.0, ((0, 32), (1, 8)))
    return dict(hidden_in=hidden_in, norm_gain=norm_gain, out_grad=out_grad, router_score=router_score, expert_ids=expert_ids, gate_saved=gate_saved, up_saved=up_saved, w_gate=w_gate, w_up=w_up, w_down=w_down, w_out=w_out, queries=queries, keys=keys, values=values)


EPSILON = 1e-05
MASKED = -1e+30

def silu_parts(gate_pre):
    sigmoid_val = jax.nn.sigmoid(gate_pre)
    return (gate_pre * sigmoid_val, sigmoid_val * (1.0 + gate_pre * (1.0 - sigmoid_val)))

def routing(expert_ids):
    chosen = expert_ids[:, 0].reshape(N_CTX, TOK_DEV)
    onehot = (chosen[:, :, None] == jnp.arange(EXPERTS, dtype=jnp.int32)[None, None, :]).astype(jnp.int32)
    before = jnp.cumsum(onehot, axis=1) - onehot
    ranked = lax.optimization_barrier(jnp.sum(before * onehot, axis=2))
    source = jnp.arange(N_CTX, dtype=jnp.int32)[:, None]
    slot_of = source * CAP + ranked
    return (chosen.reshape(TOKENS), slot_of.reshape(TOKENS).astype(jnp.int32))

def member_grads(slots_in, scores_in, gate_pre, up_pre, gate_mat, up_mat, down_mat):
    feature_width = D // N_TP
    hidden_grad = jnp.zeros((FF_GRP, SLOTS), jnp.float32)
    for slice_index in range(N_TP):
        lower = slice_index * feature_width
        term = jnp.dot(down_mat[:, lower:lower + feature_width], slots_in[:, lower:lower + feature_width].T, preferred_element_type=jnp.float32)
        term = lax.optimization_barrier(term.astype(jnp.bfloat16))
        hidden_grad = hidden_grad + term.astype(jnp.float32)
    gate_val = gate_pre.astype(jnp.float32)
    up_val = up_pre.astype(jnp.float32)
    activation, slope = silu_parts(gate_val)
    scaled = hidden_grad * scores_in[None, :]
    grad_gate = (scaled * up_val * slope).astype(jnp.bfloat16)
    grad_up = (scaled * activation).astype(jnp.bfloat16)
    router_terms = lax.optimization_barrier(jnp.sum((activation * up_val * hidden_grad).reshape(N_TP, FF_GRP // N_TP, SLOTS), axis=1))
    router_terms = lax.optimization_barrier(router_terms.astype(jnp.bfloat16)).astype(jnp.float32)
    back = jnp.dot(grad_gate.T, gate_mat.T, preferred_element_type=jnp.float32)
    back = back + jnp.dot(grad_up.T, up_mat.T, preferred_element_type=jnp.float32)
    return (back.astype(jnp.bfloat16), lax.optimization_barrier(jnp.sum(router_terms, axis=0)))

def head_grads(query_head, key_head, value_head, dout_head):
    softmax_scale = HD ** (-0.5)
    query_val = query_head.astype(jnp.float32)
    key_val = key_head.astype(jnp.float32)
    scores = jnp.dot(query_val, key_val.T, precision=lax.Precision.HIGHEST) * softmax_scale
    row_pos = jnp.arange(TOKENS, dtype=jnp.int32)[:, None]
    col_pos = jnp.arange(TOKENS, dtype=jnp.int32)[None, :]
    masked = jnp.where(col_pos <= row_pos, scores, MASKED)
    row_max = lax.optimization_barrier(jnp.max(masked, axis=1, keepdims=True))
    log_total = row_max + jnp.log(lax.optimization_barrier(jnp.sum(jnp.exp(masked - row_max), axis=1, keepdims=True)))
    prob = jnp.exp(masked - log_total)
    dprob = jnp.dot(dout_head.astype(jnp.float32), value_head.astype(jnp.float32).T, precision=lax.Precision.HIGHEST)
    delta = lax.optimization_barrier(jnp.sum(prob * dprob, axis=1, keepdims=True))
    dscore = (prob * (dprob - delta)).astype(jnp.bfloat16)
    query_out = jnp.dot(dscore, key_head, preferred_element_type=jnp.float32) * softmax_scale
    key_out = jnp.dot(dscore.T, query_head, preferred_element_type=jnp.float32) * softmax_scale
    value_out = jnp.dot(prob.astype(jnp.bfloat16).T, dout_head, preferred_element_type=jnp.float32)
    return (query_out, key_out, value_out)

def reference(hidden_in, norm_gain, out_grad, router_score, expert_ids, gate_saved, up_saved, w_gate, w_up, w_down, w_out, queries, keys, values):
    chosen, slot_of = routing(expert_ids)
    grad_slots = jnp.zeros((EXPERTS, SLOTS, D), jnp.bfloat16).at[chosen, slot_of].set(out_grad)
    score_slots = jnp.zeros((EXPERTS, SLOTS), jnp.bfloat16).at[chosen, slot_of].set(router_score)

    def one_expert(expert):
        slots_in = grad_slots[expert]
        scores_in = score_slots[expert].astype(jnp.float32)
        back_sum = jnp.zeros((SLOTS, D), jnp.float32)
        router_sum = jnp.zeros((SLOTS,), jnp.float32)
        for member in range(GROUP):
            device = expert * GROUP + member
            back_part, router_part = member_grads(slots_in, scores_in, gate_saved[device], up_saved[device], w_gate[device], w_up[device], w_down[device])
            back_sum = back_sum + back_part.astype(jnp.float32)
            router_sum = router_sum + router_part
        return (back_sum, router_sum)
    back_all, router_all = lax.map(one_expert, jnp.arange(EXPERTS, dtype=jnp.int32))
    norm_grad = back_all[chosen, slot_of]
    router_grad = router_all[chosen, slot_of]
    hidden_val = hidden_in.astype(jnp.float32)
    gain_val = norm_gain.astype(jnp.float32)[None, :]
    sum_squares = lax.optimization_barrier(jnp.sum(hidden_val * hidden_val, axis=1, keepdims=True))
    inverse_rms = lax.rsqrt(sum_squares / D + EPSILON)
    cross_sum = lax.optimization_barrier(jnp.sum(hidden_val * gain_val * norm_grad, axis=1, keepdims=True))
    d_hidden = (out_grad.astype(jnp.float32) + inverse_rms * gain_val * norm_grad - hidden_val * inverse_rms * inverse_rms * inverse_rms * cross_sum / D).astype(jnp.bfloat16)
    attn_grad = jnp.dot(d_hidden, w_out.T, preferred_element_type=jnp.float32).astype(jnp.bfloat16)
    query_heads = queries.reshape(TOKENS, QH, HD)
    key_heads = keys.reshape(TOKENS, KVH, HD)
    value_heads = values.reshape(TOKENS, KVH, HD)
    dout_heads = attn_grad.reshape(TOKENS, QH, HD)
    per_group = QH // KVH

    def one_head(head_index):
        kv_index = head_index // per_group
        return head_grads(lax.dynamic_index_in_dim(query_heads, head_index, 1, keepdims=False), lax.dynamic_index_in_dim(key_heads, kv_index, 1, keepdims=False), lax.dynamic_index_in_dim(value_heads, kv_index, 1, keepdims=False), lax.dynamic_index_in_dim(dout_heads, head_index, 1, keepdims=False))
    query_all, key_all, value_all = lax.map(one_head, jnp.arange(QH, dtype=jnp.int32))
    query_grad = jnp.transpose(query_all, (1, 0, 2)).reshape(TOKENS, QH * HD).astype(jnp.bfloat16)
    key_sum = lax.optimization_barrier(jnp.sum(key_all.reshape(KVH, per_group, TOKENS, HD), axis=1))
    value_sum = lax.optimization_barrier(jnp.sum(value_all.reshape(KVH, per_group, TOKENS, HD), axis=1))
    key_grad = jnp.transpose(key_sum, (1, 0, 2)).reshape(TOKENS, KVH * HD).astype(jnp.bfloat16)
    value_grad = jnp.transpose(value_sum, (1, 0, 2)).reshape(TOKENS, KVH * HD).astype(jnp.bfloat16)
    return (d_hidden, router_grad, query_grad, key_grad, value_grad)
```

```python
import jax
import jax.numpy as jnp
from jax import lax
from jax.experimental import pallas as pl
from jax.experimental.pallas import tpu as pltpu
from jax.sharding import PartitionSpec as P

D = 5120
QH = 40
KVH = 8
HD = 128
EXPERTS = 8
GROUP_Q = QH // KVH
N_CTX = 32
BLOCK = 128
PAIR = 2 * BLOCK
ROWS_Q = GROUP_Q * BLOCK
W_ROWS = 160
MESH = pl.DeviceIdType.MESH
EPSILON = 1e-05
NEG = -1e30
LOG2E = 1.4426950408889634


def silu_parts(gate_pre):
    sigmoid_val = jax.nn.sigmoid(gate_pre)
    return (gate_pre * sigmoid_val, sigmoid_val * (1.0 + gate_pre * (1.0 - sigmoid_val)))


def contract_last(left_mat, right_mat):
    return lax.dot_general(
        left_mat, right_mat, (((1,), (1,)), ((), ())), preferred_element_type=jnp.float32
    )


def contract_first(left_mat, right_mat):
    return lax.dot_general(
        left_mat, right_mat, (((0,), (1,)), ((), ())), preferred_element_type=jnp.float32
    )


def mm(a, b):
    return jnp.dot(a, b, preferred_element_type=jnp.float32)


def attention_kernel(
    full_ref, q_ref, gathered_ref, dq_ref, dk_ref, dv_ref,
    w_buf, k_buf, v_buf, kt_buf, qt_buf, q5_buf, dt_buf, d5_buf,
    s_buf, dp_buf, p16_buf, ds16_buf, m_buf, l_buf, r_buf, dqt_buf,
    send_buf, recv_buf, w_sem, kv_sem, send_sem, recv_sem,
):
    me = lax.axis_index("ctx")
    tp = lax.axis_index("tp")
    scale = HD ** -0.5

    barrier = pltpu.get_barrier_semaphore()

    def greet(j, carry):
        pl.semaphore_signal(barrier, inc=1, device_id=(j, tp), device_id_type=MESH)
        return carry

    lax.fori_loop(me + 1, N_CTX, greet, 0)

    w_copy = pltpu.make_async_copy(gathered_ref.at[:, pl.ds(0, ROWS_Q)], w_buf, w_sem)

    def kv_copies(j):
        rows = pl.ds(pl.multiple_of(j * W_ROWS, 32), BLOCK)
        own = pl.ds(pl.multiple_of(j * BLOCK, BLOCK), BLOCK)
        return (
            pltpu.make_async_copy(
                gathered_ref.at[rows, pl.ds(ROWS_Q, HD)], k_buf.at[own], kv_sem.at[0, j]
            ),
            pltpu.make_async_copy(
                gathered_ref.at[rows, pl.ds(ROWS_Q + HD, HD)], v_buf.at[own], kv_sem.at[1, j]
            ),
        )

    def kv_start(j, carry):
        for copy in kv_copies(j):
            copy.start()
        return carry

    lax.fori_loop(0, N_CTX, kv_start, 0)
    w_copy.start()

    for h in range(GROUP_Q):
        cols = slice(h * BLOCK, (h + 1) * BLOCK)
        head = q_ref[:, cols]
        q5_buf[cols, :] = head
        qt_buf[:, cols] = head.astype(jnp.float32).T.astype(jnp.bfloat16)

    def kv_wait(j, carry):
        for copy in kv_copies(j):
            copy.wait()
        return carry

    lax.fori_loop(0, N_CTX, kv_wait, 0)

    last = me // 2
    m_buf[...] = jnp.full(m_buf.shape, NEG, jnp.float32)
    l_buf[...] = jnp.zeros_like(l_buf)
    r_buf[...] = jnp.zeros_like(r_buf)
    dqt_buf[...] = jnp.zeros_like(dqt_buf)

    def pair_rows(p):
        return pl.ds(pl.multiple_of(p * PAIR, PAIR), PAIR)

    def fold(x, op):
        total = x[0:8]
        for i in range(1, x.shape[0] // 8):
            total = op(total, x[8 * i : 8 * i + 8])
        return total

    def score_pass(p, masked):
        keys = k_buf[pair_rows(p), :]
        kt_buf[p] = keys.astype(jnp.float32).T.astype(jnp.bfloat16)
        for n in range(GROUP_Q):
            cols = slice(n * BLOCK, (n + 1) * BLOCK)
            part = mm(keys, qt_buf[:, cols])
            if masked:
                key_pos = lax.broadcasted_iota(jnp.int32, (PAIR, BLOCK), 0)
                row_pos = lax.broadcasted_iota(jnp.int32, (PAIR, BLOCK), 1)
                part = jnp.where(key_pos <= row_pos + (me % 2) * BLOCK, part, NEG)
            s_buf[p, :, cols] = part
            m_buf[:, cols] = jnp.maximum(m_buf[:, cols], fold(part, jnp.maximum))

    def score_step(p, carry):
        score_pass(p, False)
        return carry

    lax.fori_loop(0, last, score_step, 0)
    score_pass(last, True)
    row_max = jnp.max(m_buf[...], axis=0, keepdims=True)
    m_buf[...] = jnp.broadcast_to(row_max, m_buf.shape)

    w_copy.wait()
    dout = mm(full_ref[...], w_buf[...]).astype(jnp.bfloat16)
    for h in range(GROUP_Q):
        cols = slice(h * BLOCK, (h + 1) * BLOCK)
        head = dout[:, cols]
        d5_buf[cols, :] = head
        dt_buf[:, cols] = head.astype(jnp.float32).T.astype(jnp.bfloat16)

    step_rows = 32

    def prob_step(p, carry):
        vals = v_buf[pair_rows(p), :]
        dp_buf[p] = mm(vals, dt_buf[...])
        top = m_buf[0:1, :]
        l_now = l_buf[...]
        r_now = r_buf[...]
        for i in range(PAIR // step_rows):
            rows = slice(i * step_rows, (i + 1) * step_rows)
            e = jnp.exp2((s_buf[p, rows, :] - top) * (scale * LOG2E))
            s_buf[p, rows, :] = e
            l_now = l_now + fold(e, jnp.add)
            r_now = r_now + fold(e * dp_buf[p, rows, :], jnp.add)
        l_buf[...] = l_now
        r_buf[...] = r_now
        return carry

    lax.fori_loop(0, last + 1, prob_step, 0)
    row_sum = jnp.sum(l_buf[...], axis=0, keepdims=True)
    inverse = 1.0 / row_sum
    delta = jnp.sum(r_buf[...], axis=0, keepdims=True) * inverse

    @pl.when(me > 0)
    def _():
        pl.semaphore_wait(barrier, me)

    def sent(j):
        return pltpu.make_async_remote_copy(
            src_ref=send_buf.at[j],
            dst_ref=recv_buf.at[me],
            send_sem=send_sem.at[j],
            recv_sem=recv_sem.at[me],
            device_id=(j, tp),
            device_id_type=MESH,
        )

    def grad_step(p, carry):
        for i in range(PAIR // step_rows):
            rows = slice(i * step_rows, (i + 1) * step_rows)
            prob = s_buf[p, rows, :] * inverse
            p16_buf[rows, :] = prob.astype(jnp.bfloat16)
            ds16_buf[rows, :] = (prob * (dp_buf[p, rows, :] - delta)).astype(jnp.bfloat16)
        ds16 = ds16_buf[...]
        dk = (mm(ds16, q5_buf[...]) * scale).astype(jnp.bfloat16)
        dv = mm(p16_buf[...], d5_buf[...]).astype(jnp.bfloat16)
        dqt_buf[...] += mm(kt_buf[p], ds16)
        for half in range(2):
            j = 2 * p + half
            rows = slice(half * BLOCK, (half + 1) * BLOCK)
            send_buf[j, 0:BLOCK, :] = dk[rows]
            send_buf[j, BLOCK:PAIR, :] = dv[rows]

            @pl.when(j < me)
            def _():
                sent(j).start()

        return carry

    lax.fori_loop(0, last + 1, grad_step, 0)

    for h in range(GROUP_Q):
        cols = slice(h * BLOCK, (h + 1) * BLOCK)
        dq_ref[:, cols] = (dqt_buf[:, cols].T * scale).astype(jnp.bfloat16)

    dk_ref[...] = send_buf[me, 0:BLOCK, :].astype(jnp.float32)
    dv_ref[...] = send_buf[me, BLOCK:PAIR, :].astype(jnp.float32)

    def take(j, carry):
        pltpu.make_async_remote_copy(
            src_ref=send_buf.at[j],
            dst_ref=recv_buf.at[j],
            send_sem=send_sem.at[j],
            recv_sem=recv_sem.at[j],
            device_id=(j, tp),
            device_id_type=MESH,
        ).wait_recv()
        dk_ref[...] += recv_buf[j, 0:BLOCK, :].astype(jnp.float32)
        dv_ref[...] += recv_buf[j, BLOCK:PAIR, :].astype(jnp.float32)
        return carry

    lax.fori_loop(me + 1, N_CTX, take, 0)

    def drain(j, carry):
        sent(j).wait_send()
        return carry

    lax.fori_loop(0, me, drain, 0)


def attention(full_grad, queries, gathered):
    pairs = N_CTX // 2
    bf, f32 = jnp.bfloat16, jnp.float32
    vmem = pl.BlockSpec(memory_space=pltpu.VMEM)
    return pl.pallas_call(
        attention_kernel,
        name="attention_grads",
        out_shape=[
            jax.ShapeDtypeStruct((BLOCK, ROWS_Q), bf),
            jax.ShapeDtypeStruct((BLOCK, HD), f32),
            jax.ShapeDtypeStruct((BLOCK, HD), f32),
        ],
        in_specs=[vmem, vmem, pl.BlockSpec(memory_space=pl.ANY)],
        out_specs=[vmem, vmem, vmem],
        scratch_shapes=[
            pltpu.VMEM((D, ROWS_Q), bf),
            pltpu.VMEM((N_CTX * BLOCK, HD), bf),
            pltpu.VMEM((N_CTX * BLOCK, HD), bf),
            pltpu.VMEM((pairs, HD, PAIR), bf),
            pltpu.VMEM((HD, ROWS_Q), bf),
            pltpu.VMEM((ROWS_Q, HD), bf),
            pltpu.VMEM((HD, ROWS_Q), bf),
            pltpu.VMEM((ROWS_Q, HD), bf),
            pltpu.VMEM((pairs, PAIR, ROWS_Q), f32),
            pltpu.VMEM((pairs, PAIR, ROWS_Q), f32),
            pltpu.VMEM((PAIR, ROWS_Q), bf),
            pltpu.VMEM((PAIR, ROWS_Q), bf),
            pltpu.VMEM((8, ROWS_Q), f32),
            pltpu.VMEM((8, ROWS_Q), f32),
            pltpu.VMEM((8, ROWS_Q), f32),
            pltpu.VMEM((HD, ROWS_Q), f32),
            pltpu.VMEM((N_CTX, PAIR, HD), bf),
            pltpu.VMEM((N_CTX, PAIR, HD), bf),
            pltpu.SemaphoreType.DMA,
            pltpu.SemaphoreType.DMA((2, N_CTX)),
            pltpu.SemaphoreType.DMA((N_CTX,)),
            pltpu.SemaphoreType.DMA((N_CTX,)),
        ],
        cost_estimate=pl.CostEstimate(
            flops=6_000_000_000, bytes_accessed=12_000_000, transcendentals=3_000_000
        ),
        compiler_params=pltpu.CompilerParams(
            collective_id=4, has_side_effects=True, vmem_limit_bytes=56 * 2**20
        ),
    )(full_grad, queries, gathered)


def body(
    hidden_in,
    norm_gain,
    out_grad,
    router_score,
    expert_ids,
    gate_saved,
    up_saved,
    w_gate,
    w_up,
    w_down,
    w_out,
    queries,
    keys,
    values,
):
    devices = lax.axis_size("ctx")
    sharing = devices // EXPERTS
    tok_rows, feature_cols = out_grad.shape
    capacity = gate_saved.shape[2] // devices

    pad = W_ROWS - tok_rows
    shared_part = jnp.concatenate(
        [w_out.T, jnp.pad(keys, ((0, pad), (0, 0))), jnp.pad(values, ((0, pad), (0, 0)))], axis=1
    )
    gathered = lax.all_gather(shared_part, "ctx", axis=0, tiled=True)

    chosen = expert_ids[:, 0]
    onehot = (chosen[:, None] == jnp.arange(EXPERTS, dtype=jnp.int32)[None, :]).astype(jnp.int32)
    ranked = jnp.sum((jnp.cumsum(onehot, axis=0) - onehot) * onehot, axis=1)
    slot_index = chosen * capacity + ranked
    placing = (
        jnp.arange(EXPERTS * capacity, dtype=jnp.int32)[:, None] == slot_index[None, :]
    ).astype(jnp.bfloat16)
    grad_slots = jnp.dot(placing, out_grad, preferred_element_type=jnp.float32).astype(jnp.bfloat16)
    score_slots = jnp.dot(
        placing, router_score[:, None], preferred_element_type=jnp.float32
    ).astype(jnp.bfloat16)
    sent_grad = jnp.repeat(grad_slots.reshape(EXPERTS, capacity, feature_cols), sharing, axis=0)
    sent_score = jnp.repeat(score_slots.reshape(EXPERTS, capacity), sharing, axis=0)
    arrived, arrived_score = (
        lax.all_to_all(sent_grad, "ctx", split_axis=0, concat_axis=0, tiled=True),
        lax.all_to_all(sent_score, "ctx", split_axis=0, concat_axis=0, tiled=True),
    )
    slot_grad = arrived.reshape(devices * capacity, feature_cols)
    slot_score = arrived_score.reshape(devices * capacity).astype(jnp.float32)
    down_local = w_down[0]
    hidden_grad = lax.psum_scatter(
        contract_last(down_local, slot_grad).astype(jnp.bfloat16),
        "tp",
        scatter_dimension=0,
        tiled=True,
    ).astype(jnp.float32)
    gate_val = gate_saved[0].astype(jnp.float32)
    up_val = up_saved[0].astype(jnp.float32)
    activation, slope = silu_parts(gate_val)
    scaled = hidden_grad * slot_score[None, :]
    grad_gate = (scaled * up_val * slope).astype(jnp.bfloat16)
    grad_up = (scaled * activation).astype(jnp.bfloat16)
    router_part = jnp.sum(activation * up_val * hidden_grad, axis=0).astype(jnp.bfloat16)
    gate_local = w_gate[0]
    up_local = w_up[0]
    running = contract_first(lax.all_gather(grad_gate, "tp", axis=0, tiled=True), gate_local)
    back = running + contract_first(lax.all_gather(grad_up, "tp", axis=0, tiled=True), up_local)
    back_parts = back.astype(jnp.bfloat16).reshape(devices, capacity, feature_cols)
    returned, returned_router = (
        lax.all_to_all(back_parts, "ctx", split_axis=0, concat_axis=0, tiled=True),
        lax.all_to_all(
            router_part.reshape(devices, capacity), "ctx", split_axis=0, concat_axis=0, tiled=True
        ),
    )
    summed = jnp.sum(
        returned.astype(jnp.float32).reshape(EXPERTS, sharing, capacity, feature_cols), axis=1
    ).reshape(EXPERTS * capacity, feature_cols)
    router_sum = jnp.sum(
        returned_router.astype(jnp.float32).reshape(EXPERTS, sharing, capacity), axis=1
    ).reshape(EXPERTS * capacity)
    norm_grad = jnp.take(summed, slot_index, axis=0)
    router_tok = jnp.take(router_sum, slot_index, axis=0)
    hidden_val = hidden_in.astype(jnp.float32)
    gain_val = norm_gain.astype(jnp.float32)[None, :]
    squares_part = jnp.sum(hidden_val * hidden_val, axis=1)
    cross_part = jnp.sum(hidden_val * gain_val * norm_grad, axis=1)
    router_grad, sum_squares, cross_sum = lax.psum((router_tok, squares_part, cross_part), "tp")
    inverse_rms = lax.rsqrt(sum_squares / D + EPSILON)[:, None]
    d_hidden = (
        out_grad.astype(jnp.float32)
        + inverse_rms * gain_val * norm_grad
        - hidden_val * inverse_rms * inverse_rms * inverse_rms * cross_sum[:, None] / D
    ).astype(jnp.bfloat16)
    full_grad = lax.all_gather(d_hidden, "tp", axis=1, tiled=True)
    query_grad, key_grad, value_grad = attention(full_grad, queries, gathered)
    return (
        d_hidden,
        router_grad,
        query_grad,
        key_grad.astype(jnp.bfloat16),
        value_grad.astype(jnp.bfloat16),
    )


def solution(mesh):
    in_specs = (
        P("ctx", "tp"),
        P("tp"),
        P("ctx", "tp"),
        P("ctx"),
        P("ctx", None),
        P("ctx", "tp", None),
        P("ctx", "tp", None),
        P("ctx", "tp", None),
        P("ctx", "tp", None),
        P("ctx", None, "tp"),
        P("tp", "ctx"),
        P("ctx", "tp"),
        P("ctx", "tp"),
        P("ctx", "tp"),
    )
    out_specs = (P("ctx", "tp"), P("ctx"), P("ctx", "tp"), P("ctx", "tp"), P("ctx", "tp"))
    return jax.shard_map(body, mesh=mesh, in_specs=in_specs, out_specs=out_specs, check_vma=False)
```

```python
import jax
import jax.numpy as jnp
from jax import lax
from jax.experimental import pallas as pl
from jax.experimental.pallas import tpu as pltpu
from jax.sharding import PartitionSpec as P

D = 5120
QH = 40
KVH = 8
HD = 128
EXPERTS = 8
GROUP_Q = QH // KVH
N_CTX = 32
BLOCK = 128
PAIR = 2 * BLOCK
ROWS_Q = GROUP_Q * BLOCK
W_ROWS = 160
N_Y, N_Z, N_X, N_TP = 4, 8, 4, 8
GROUP = N_CTX // EXPERTS
CAP = 24
CAP_PAD = 32
CHUNK = N_Z * CAP
SLOTS = N_CTX * CAP
FEAT = D // N_TP
FF_GRP = 2048
FF_DEV = FF_GRP // N_TP
ROW_ORDER = (0, 1, 3, 2)
MESH = pl.DeviceIdType.MESH
EPSILON = 1e-05
NEG = -1e30
LOG2E = 1.4426950408889634


def silu_parts(gate_pre):
    sigmoid_val = jax.nn.sigmoid(gate_pre)
    return (gate_pre * sigmoid_val, sigmoid_val * (1.0 + gate_pre * (1.0 - sigmoid_val)))


def mm(a, b):
    return jnp.dot(a, b, preferred_element_type=jnp.float32)


def attention_kernel(
    full_ref, q_ref, gathered_ref, dq_ref, dk_ref, dv_ref,
    w_buf, k_buf, v_buf, kt_buf, qt_buf, q5_buf, dt_buf, d5_buf,
    s_buf, dp_buf, p16_buf, ds16_buf, m_buf, l_buf, r_buf, dqt_buf,
    send_buf, recv_buf, total_buf, w_sem, kv_sem, send_sem, recv_sem,
):
    me = lax.axis_index("ctx")
    tp = lax.axis_index("tp")
    scale = HD ** -0.5

    barrier = pltpu.get_barrier_semaphore()

    def greet(j, carry):
        pl.semaphore_signal(barrier, inc=1, device_id=(j, tp), device_id_type=MESH)
        return carry

    lax.fori_loop(me + 1, N_CTX, greet, 0)

    w_copy = pltpu.make_async_copy(gathered_ref.at[:, pl.ds(0, ROWS_Q)], w_buf, w_sem)

    def kv_copies(j):
        rows = pl.ds(pl.multiple_of(j * W_ROWS, 32), BLOCK)
        own = pl.ds(pl.multiple_of(j * BLOCK, BLOCK), BLOCK)
        return (
            pltpu.make_async_copy(
                gathered_ref.at[rows, pl.ds(ROWS_Q, HD)], k_buf.at[own], kv_sem.at[0, j]
            ),
            pltpu.make_async_copy(
                gathered_ref.at[rows, pl.ds(ROWS_Q + HD, HD)], v_buf.at[own], kv_sem.at[1, j]
            ),
        )

    def kv_start(j, carry):
        for copy in kv_copies(j):
            copy.start()
        return carry

    lax.fori_loop(0, N_CTX, kv_start, 0)
    w_copy.start()

    for h in range(GROUP_Q):
        cols = slice(h * BLOCK, (h + 1) * BLOCK)
        head = q_ref[:, cols]
        q5_buf[cols, :] = head
        qt_buf[:, cols] = head.astype(jnp.float32).T.astype(jnp.bfloat16)

    def kv_wait(j, carry):
        for copy in kv_copies(j):
            copy.wait()
        return carry

    lax.fori_loop(0, N_CTX, kv_wait, 0)

    last = me // 2
    m_buf[...] = jnp.full(m_buf.shape, NEG, jnp.float32)
    l_buf[...] = jnp.zeros_like(l_buf)
    r_buf[...] = jnp.zeros_like(r_buf)
    dqt_buf[...] = jnp.zeros_like(dqt_buf)

    def pair_rows(p):
        return pl.ds(pl.multiple_of(p * PAIR, PAIR), PAIR)

    def fold(x, op):
        total = x[0:8]
        for i in range(1, x.shape[0] // 8):
            total = op(total, x[8 * i : 8 * i + 8])
        return total

    def score_pass(p, masked):
        keys = k_buf[pair_rows(p), :]
        kt_buf[p] = keys.astype(jnp.float32).T.astype(jnp.bfloat16)
        for n in range(GROUP_Q):
            cols = slice(n * BLOCK, (n + 1) * BLOCK)
            part = mm(keys, qt_buf[:, cols])
            if masked:
                key_pos = lax.broadcasted_iota(jnp.int32, (PAIR, BLOCK), 0)
                row_pos = lax.broadcasted_iota(jnp.int32, (PAIR, BLOCK), 1)
                part = jnp.where(key_pos <= row_pos + (me % 2) * BLOCK, part, NEG)
            s_buf[p, :, cols] = part
            m_buf[:, cols] = jnp.maximum(m_buf[:, cols], fold(part, jnp.maximum))

    def score_step(p, carry):
        score_pass(p, False)
        return carry

    lax.fori_loop(0, last, score_step, 0)
    score_pass(last, True)
    row_max = jnp.max(m_buf[...], axis=0, keepdims=True)
    m_buf[...] = jnp.broadcast_to(row_max, m_buf.shape)

    w_copy.wait()
    dout = mm(full_ref[0], w_buf[0:FEAT, :])
    for t in range(1, N_TP):
        dout = dout + mm(full_ref[t], w_buf[t * FEAT : (t + 1) * FEAT, :])
    dout = dout.astype(jnp.bfloat16)
    for h in range(GROUP_Q):
        cols = slice(h * BLOCK, (h + 1) * BLOCK)
        head = dout[:, cols]
        d5_buf[cols, :] = head
        dt_buf[:, cols] = head.astype(jnp.float32).T.astype(jnp.bfloat16)

    step_rows = 32

    def prob_step(p, carry):
        vals = v_buf[pair_rows(p), :]
        dp_buf[p] = mm(vals, dt_buf[...])
        top = m_buf[0:1, :]
        l_now = l_buf[...]
        r_now = r_buf[...]
        for i in range(PAIR // step_rows):
            rows = slice(i * step_rows, (i + 1) * step_rows)
            e = jnp.exp2((s_buf[p, rows, :] - top) * (scale * LOG2E))
            s_buf[p, rows, :] = e
            l_now = l_now + fold(e, jnp.add)
            r_now = r_now + fold(e * dp_buf[p, rows, :], jnp.add)
        l_buf[...] = l_now
        r_buf[...] = r_now
        return carry

    lax.fori_loop(0, last + 1, prob_step, 0)
    row_sum = jnp.sum(l_buf[...], axis=0, keepdims=True)
    inverse = 1.0 / row_sum
    delta = jnp.sum(r_buf[...], axis=0, keepdims=True) * inverse

    @pl.when(me > 0)
    def _():
        pl.semaphore_wait(barrier, me)

    def sent(j):
        return pltpu.make_async_remote_copy(
            src_ref=send_buf.at[j],
            dst_ref=recv_buf.at[me],
            send_sem=send_sem.at[j],
            recv_sem=recv_sem.at[me],
            device_id=(j, tp),
            device_id_type=MESH,
        )

    def grad_step(p, carry):
        for i in range(PAIR // step_rows):
            rows = slice(i * step_rows, (i + 1) * step_rows)
            prob = s_buf[p, rows, :] * inverse
            p16_buf[rows, :] = prob.astype(jnp.bfloat16)
            ds16_buf[rows, :] = (prob * (dp_buf[p, rows, :] - delta)).astype(jnp.bfloat16)
        ds16 = ds16_buf[...]
        dk = (mm(ds16, q5_buf[...]) * scale).astype(jnp.bfloat16)
        dv = mm(p16_buf[...], d5_buf[...]).astype(jnp.bfloat16)
        dqt_buf[...] += mm(kt_buf[p], ds16)
        for half in range(2):
            j = 2 * p + half
            rows = slice(half * BLOCK, (half + 1) * BLOCK)
            send_buf[j, 0:BLOCK, :] = dk[rows]
            send_buf[j, BLOCK:PAIR, :] = dv[rows]

            @pl.when(j < me)
            def _():
                sent(j).start()

        return carry

    lax.fori_loop(0, last + 1, grad_step, 0)

    for h in range(GROUP_Q):
        cols = slice(h * BLOCK, (h + 1) * BLOCK)
        dq_ref[:, cols] = (dqt_buf[:, cols].T * scale).astype(jnp.bfloat16)

    total_buf[...] = send_buf[me].astype(jnp.float32)

    def take(j, carry):
        pltpu.make_async_remote_copy(
            src_ref=send_buf.at[j],
            dst_ref=recv_buf.at[j],
            send_sem=send_sem.at[j],
            recv_sem=recv_sem.at[j],
            device_id=(j, tp),
            device_id_type=MESH,
        ).wait_recv()
        total_buf[...] += recv_buf[j].astype(jnp.float32)
        return carry

    lax.fori_loop(me + 1, N_CTX, take, 0)
    dk_ref[...] = total_buf[0:BLOCK, :].astype(jnp.bfloat16)
    dv_ref[...] = total_buf[BLOCK:PAIR, :].astype(jnp.bfloat16)

    def drain(j, carry):
        sent(j).wait_send()
        return carry

    lax.fori_loop(0, me, drain, 0)


def attention(full_grad, queries, gathered):
    pairs = N_CTX // 2
    bf, f32 = jnp.bfloat16, jnp.float32
    vmem = pl.BlockSpec(memory_space=pltpu.VMEM)
    return pl.pallas_call(
        attention_kernel,
        name="attention_grads",
        out_shape=[
            jax.ShapeDtypeStruct((BLOCK, ROWS_Q), bf),
            jax.ShapeDtypeStruct((BLOCK, HD), bf),
            jax.ShapeDtypeStruct((BLOCK, HD), bf),
        ],
        in_specs=[vmem, vmem, pl.BlockSpec(memory_space=pl.ANY)],
        out_specs=[vmem, vmem, vmem],
        scratch_shapes=[
            pltpu.VMEM((D, ROWS_Q), bf),
            pltpu.VMEM((N_CTX * BLOCK, HD), bf),
            pltpu.VMEM((N_CTX * BLOCK, HD), bf),
            pltpu.VMEM((pairs, HD, PAIR), bf),
            pltpu.VMEM((HD, ROWS_Q), bf),
            pltpu.VMEM((ROWS_Q, HD), bf),
            pltpu.VMEM((HD, ROWS_Q), bf),
            pltpu.VMEM((ROWS_Q, HD), bf),
            pltpu.VMEM((pairs, PAIR, ROWS_Q), f32),
            pltpu.VMEM((pairs, PAIR, ROWS_Q), f32),
            pltpu.VMEM((PAIR, ROWS_Q), bf),
            pltpu.VMEM((PAIR, ROWS_Q), bf),
            pltpu.VMEM((8, ROWS_Q), f32),
            pltpu.VMEM((8, ROWS_Q), f32),
            pltpu.VMEM((8, ROWS_Q), f32),
            pltpu.VMEM((HD, ROWS_Q), f32),
            pltpu.VMEM((N_CTX, PAIR, HD), bf),
            pltpu.VMEM((N_CTX, PAIR, HD), bf),
            pltpu.VMEM((PAIR, HD), f32),
            pltpu.SemaphoreType.DMA,
            pltpu.SemaphoreType.DMA((2, N_CTX)),
            pltpu.SemaphoreType.DMA((N_CTX,)),
            pltpu.SemaphoreType.DMA((N_CTX,)),
        ],
        cost_estimate=pl.CostEstimate(
            flops=6_000_000_000, bytes_accessed=12_000_000, transcendentals=3_000_000
        ),
        compiler_params=pltpu.CompilerParams(
            collective_id=4, has_side_effects=True, vmem_limit_bytes=56 * 2**20
        ),
    )(full_grad, queries, gathered)


def dot_nt(a, b):
    return lax.dot_general(a, b, (((1,), (1,)), ((), ())), preferred_element_type=jnp.float32)


def expert_kernel(
    slots_ref, pick_ref, score_ref, hidden_ref, gain_ref, grad_ref,
    down_ref, gate_ref, up_ref, wg_ref, wu_ref,
    dh_ref, stat_ref, full_ref,
    down, wg, wu, recv_d, flat, slots, own, sib_out, sib_in, x_out, x_in,
    act_buf, slope_buf, prod_buf, ag, acc, back, ret, picked, stats, square, full,
    w_sem, d_send, d_recv, s_send, s_recv, x_send, x_recv, ax_send, ax_recv,
    as_send, as_recv, b_send, b_recv, t_send, t_recv, fx_send, fx_recv, fs_send, fs_recv,
):
    me = lax.axis_index("ctx")
    tp = lax.axis_index("tp")
    y, z = me // N_Z, me % N_Z
    x, k = tp // 2, tp % 2
    sibling = 2 * x + (1 - k)
    far = (2, 1, 3)

    def chip(dx):
        return (x + dx) % N_X

    def remote(src, dst, send, recv, ctx, peer):
        return pltpu.make_async_remote_copy(
            src_ref=src, dst_ref=dst, send_sem=send, recv_sem=recv,
            device_id=(ctx, peer), device_id_type=MESH,
        )

    w_copies = [
        pltpu.make_async_copy(down_ref, down, w_sem.at[0]),
        pltpu.make_async_copy(wg_ref, wg, w_sem.at[1]),
        pltpu.make_async_copy(wu_ref, wu, w_sem.at[2]),
    ]
    for copy in w_copies:
        copy.start()

    barrier = pltpu.get_barrier_semaphore()

    def greet_ctx(i, carry):
        pl.semaphore_signal(
            barrier, inc=1, device_id=((me + i) % N_CTX, tp), device_id_type=MESH
        )
        return carry

    def greet_tp(i, carry):
        pl.semaphore_signal(
            barrier, inc=1, device_id=(me, (tp + i) % N_TP), device_id_type=MESH
        )
        return carry

    lax.fori_loop(1, N_CTX, greet_ctx, 0)
    lax.fori_loop(1, N_TP, greet_tp, 0)
    hidden_val = hidden_ref[...].astype(jnp.float32)
    square[...] = jnp.broadcast_to(
        jnp.sum(hidden_val * hidden_val, axis=1, keepdims=True), square.shape
    )
    pl.semaphore_wait(barrier, N_CTX - 1 + N_TP - 1)

    def dispatch(j):
        return remote(
            slots_ref.at[j // GROUP], recv_d.at[me], d_send.at[j], d_recv.at[me], j, tp
        )

    for dy in ROW_ORDER:
        row = (y - dy + N_Y) % N_Y

        def send_step(dz, carry, row=row):
            dispatch(row * N_Z + (z + dz) % N_Z).start()
            return carry

        lax.fori_loop(1 if dy == 0 else 0, N_Z, send_step, 0)
    recv_d[me] = slots_ref[me // GROUP]

    def chunk_rows(ch):
        start = ((y + ROW_ORDER[ch]) % N_Y) * CHUNK
        return pl.ds(pl.multiple_of(start, CHUNK), CHUNK)

    def arrive(ch):
        first = ((y + ROW_ORDER[ch]) % N_Y) * N_Z
        for i in range(N_Z):
            j = first + i

            @pl.when(j != me)
            def _():
                remote(
                    slots_ref.at[0], recv_d.at[j], d_send.at[j], d_recv.at[j], j, tp
                ).wait_recv()

            flat[i * CAP : (i + 1) * CAP, :] = recv_d[j].astype(jnp.float32)
        slots[chunk_rows(ch), :] = flat[...].astype(jnp.bfloat16)

    def sib_copy(i, ch):
        rows = chunk_rows(ch)
        return remote(
            sib_out.at[i, rows], sib_in.at[i, rows], s_send.at[i, ch], s_recv.at[i, ch],
            me, sibling,
        )

    def x_copy(i, ch):
        rows = chunk_rows(ch)
        return remote(
            x_out.at[i, rows], x_in.at[i, rows], x_send.at[i, ch], x_recv.at[i, ch],
            me, 2 * chip(far[i]) + k,
        )

    def stage1(ch):
        rows = chunk_rows(ch)
        part = slots[rows, :]
        for i, dx in enumerate(far + (0,)):
            base = 2 * chip(dx)

            def block(t):
                start = pl.multiple_of(t * FF_DEV, FF_DEV)
                return dot_nt(part, down[pl.ds(start, FF_DEV), :]).astype(jnp.bfloat16)

            sib_out[i, rows, :] = block(base + 1 - k)
            sib_copy(i, ch).start()
            own[i, rows, :] = block(base + k)

    def joined(i, ch):
        rows = chunk_rows(ch)
        sib_copy(i, ch).wait_recv()
        return own[i, rows, :].astype(jnp.float32) + sib_in[i, rows, :].astype(jnp.float32)

    def stage2(ch):
        rows = chunk_rows(ch)
        for i in range(3):
            x_out[i, rows, :] = joined(i, ch).astype(jnp.bfloat16)
            x_copy(i, ch).start()

    def prepare():
        gate = gate_ref[...].astype(jnp.float32).T
        up = up_ref[...].astype(jnp.float32).T
        act, slope = silu_parts(gate)
        act_buf[...] = act
        slope_buf[...] = up * slope
        prod_buf[...] = act * up

    def ag_out(i, ch):
        rows = chunk_rows(ch)
        return remote(
            ag.at[tp, rows], ag.at[tp, rows], ax_send.at[i, ch], ax_recv.at[i, ch],
            me, 2 * chip(far[i]) + k,
        )

    def ag_chip(i, ch):
        return 2 * chip(N_X - far[i]) + k

    def ag_in(i, ch):
        rows = chunk_rows(ch)
        t = ag_chip(i, ch)
        return remote(
            ag.at[t, rows], ag.at[t, rows], ax_send.at[i, ch], ax_recv.at[i, ch], me, t
        )

    def ag_share(t, i, ch):
        rows = chunk_rows(ch)
        return remote(
            ag.at[t, rows], ag.at[t, rows], as_send.at[i, ch], as_recv.at[i, ch], me, sibling
        )

    def stage3(ch):
        rows = chunk_rows(ch)
        hid = joined(3, ch)
        for i in range(3):
            x_copy(i, ch).wait_recv()
            hid = hid + x_in[i, rows, :].astype(jnp.float32)
        ag[tp, rows, 0:FF_DEV] = (hid * slope_buf[rows, :]).astype(jnp.bfloat16)
        ag[tp, rows, FF_DEV : 2 * FF_DEV] = (hid * act_buf[rows, :]).astype(jnp.bfloat16)
        for i in range(3):
            ag_out(i, ch).start()
        ag_share(tp, 3, ch).start()
        term = jnp.sum(hid * prod_buf[rows, :], axis=1, keepdims=True)
        prod_buf[rows, 0:HD] = jnp.broadcast_to(term, (CHUNK, HD))

    def product(t, rows):
        cols = pl.ds(pl.multiple_of(t * FF_DEV, FF_DEV), FF_DEV)
        return dot_nt(ag[t, rows, 0:FF_DEV], wg[:, cols]) + dot_nt(
            ag[t, rows, FF_DEV : 2 * FF_DEV], wu[:, cols]
        )

    def back_copy(j):
        return remote(back.at[j], ret.at[me], b_send.at[j], b_recv.at[me], j, tp)

    def stage4(ch):
        rows = chunk_rows(ch)
        acc[:, FEAT : FEAT + HD] = prod_buf[rows, 0:HD]
        acc[:, 0:FEAT] = product(tp, rows)
        for i in (1, 2, 0):
            ag_in(i, ch).wait_recv()
            ag_share(ag_chip(i, ch), i, ch).start()
            acc[:, 0:FEAT] += product(ag_chip(i, ch), rows)
        for i in (3, 1, 2, 0):
            t = sibling if i == 3 else ag_chip(i, ch) + 1 - 2 * k
            ag_share(t, i, ch).wait_recv()
            acc[:, 0:FEAT] += product(t, rows)
        first = ((y + ROW_ORDER[ch]) % N_Y) * N_Z
        for i in range(N_Z):
            j = first + i
            back[j] = acc[i * CAP : (i + 1) * CAP, :].astype(jnp.bfloat16)

            @pl.when(j != me)
            def _():
                back_copy(j).start()

    w_copies[0].wait()
    arrive(0)
    stage1(0)
    arrive(1)
    stage1(1)
    stage2(0)
    arrive(2)
    stage1(2)
    stage2(1)
    arrive(3)
    stage1(3)
    stage2(2)
    stage2(3)
    prepare()
    w_copies[1].wait()
    w_copies[2].wait()
    for ch in range(N_Y):
        stage3(ch)
    for ch in range(N_Y):
        stage4(ch)
    ret[me] = back[me]

    picked[...] = jnp.zeros_like(picked)
    for ch in range(N_Y):
        first = ((y - ROW_ORDER[ch] + N_Y) % N_Y) * N_Z
        for i in range(N_Z):
            j = first + i

            @pl.when(j != me)
            def _():
                remote(back.at[j], ret.at[j], b_send.at[j], b_recv.at[j], j, tp).wait_recv()

            acc[i * CAP : (i + 1) * CAP, :] = ret[j].astype(jnp.float32)
        cols = pl.ds(pl.multiple_of(first * CAP_PAD, N_Z * CAP_PAD), N_Z * CAP_PAD)
        picked[...] += mm(pick_ref[:, cols][:, 0:CHUNK], acc[...].astype(jnp.bfloat16))

    norm_grad = picked[:, 0:FEAT] * score_ref[...]
    hidden_now = hidden_ref[...].astype(jnp.float32)
    gain_val = gain_ref[...].astype(jnp.float32)
    cross = jnp.sum(hidden_now * gain_val * norm_grad, axis=1, keepdims=True)
    lane = lax.broadcasted_iota(jnp.int32, (BLOCK, HD), 1)
    packed = jnp.where(
        lane == 0, picked[:, FEAT : FEAT + HD], jnp.where(lane == 1, square[...], cross)
    )
    stats[tp] = packed.T[0:8, :]

    def stat_copy(peer, src):
        return remote(
            stats.at[src], stats.at[src], t_send.at[peer], t_recv.at[src], me, peer
        )

    def stat_start(i, carry):
        stat_copy((tp + i) % N_TP, tp).start()
        return carry

    def stat_wait(i, carry):
        stat_copy((tp + i) % N_TP, (tp + i) % N_TP).wait_recv()
        return carry

    lax.fori_loop(1, N_TP, stat_start, 0)
    lax.fori_loop(1, N_TP, stat_wait, 0)
    total = stats[0]
    for t in range(1, N_TP):
        total = total + stats[t]
    stat_ref[...] = total
    spread = jnp.concatenate([total] * (BLOCK // 8), axis=0).T
    inverse_rms = lax.rsqrt(spread[:, 1:2] / D + EPSILON)
    cross_sum = spread[:, 2:3]
    d_hidden = (
        grad_ref[...].astype(jnp.float32)
        + inverse_rms * gain_val * norm_grad
        - hidden_now * inverse_rms * inverse_rms * inverse_rms * cross_sum / D
    ).astype(jnp.bfloat16)
    dh_ref[...] = d_hidden
    full[tp] = d_hidden

    def full_out(i):
        return remote(
            full.at[tp], full.at[tp], fx_send.at[i], fx_recv.at[i], me, 2 * chip(far[i]) + k
        )

    def full_in(i):
        t = ag_chip(i, 0)
        return remote(full.at[t], full.at[t], fx_send.at[i], fx_recv.at[i], me, t)

    def full_share(t, i):
        return remote(full.at[t], full.at[t], fs_send.at[i], fs_recv.at[i], me, sibling)

    for i in range(3):
        full_out(i).start()
    full_share(tp, 3).start()
    for i in (1, 2, 0):
        full_in(i).wait_recv()
        full_share(ag_chip(i, 0), i).start()
    for i in (3, 1, 2, 0):
        t = sibling if i == 3 else ag_chip(i, 0) + 1 - 2 * k
        full_share(t, i).wait_recv()
    full_ref[...] = full[...]

    def drain_ctx(i, carry):
        j = (me + i) % N_CTX
        dispatch(j).wait_send()
        back_copy(j).wait_send()
        return carry

    def drain_tp(i, carry):
        stat_copy((tp + i) % N_TP, tp).wait_send()
        return carry

    lax.fori_loop(1, N_CTX, drain_ctx, 0)
    lax.fori_loop(1, N_TP, drain_tp, 0)
    for ch in range(N_Y):
        for i in range(4):
            sib_copy(i, ch).wait_send()
            ag_share(tp, i, ch).wait_send()
        for i in range(3):
            x_copy(i, ch).wait_send()
            ag_out(i, ch).wait_send()
    for i in range(3):
        full_out(i).wait_send()
    for i in range(4):
        full_share(tp, i).wait_send()


def expert_block(slots, pick, score, hidden, gain, grad, down, gate, up, wg, wu):
    bf, f32 = jnp.bfloat16, jnp.float32
    vmem = pl.BlockSpec(memory_space=pltpu.VMEM)
    hbm = pl.BlockSpec(memory_space=pl.ANY)
    dma = pltpu.SemaphoreType.DMA
    wide = FEAT + HD
    return pl.pallas_call(
        expert_kernel,
        name="expert_block",
        out_shape=[
            jax.ShapeDtypeStruct((BLOCK, FEAT), bf),
            jax.ShapeDtypeStruct((8, BLOCK), f32),
            jax.ShapeDtypeStruct((N_TP, BLOCK, FEAT), bf),
        ],
        in_specs=[vmem] * 6 + [hbm, vmem, vmem, hbm, hbm],
        out_specs=[vmem] * 3,
        scratch_shapes=[
            pltpu.VMEM((FF_GRP, FEAT), bf),
            pltpu.VMEM((FEAT, FF_GRP), bf),
            pltpu.VMEM((FEAT, FF_GRP), bf),
            pltpu.VMEM((N_CTX, CAP, FEAT), bf),
            pltpu.VMEM((CHUNK, FEAT), f32),
            pltpu.VMEM((SLOTS, FEAT), bf),
            pltpu.VMEM((4, SLOTS, FF_DEV), bf),
            pltpu.VMEM((4, SLOTS, FF_DEV), bf),
            pltpu.VMEM((4, SLOTS, FF_DEV), bf),
            pltpu.VMEM((3, SLOTS, FF_DEV), bf),
            pltpu.VMEM((3, SLOTS, FF_DEV), bf),
            pltpu.VMEM((SLOTS, FF_DEV), f32),
            pltpu.VMEM((SLOTS, FF_DEV), f32),
            pltpu.VMEM((SLOTS, FF_DEV), f32),
            pltpu.VMEM((N_TP, SLOTS, 2 * FF_DEV), bf),
            pltpu.VMEM((CHUNK, wide), f32),
            pltpu.VMEM((N_CTX, CAP, wide), bf),
            pltpu.VMEM((N_CTX, CAP, wide), bf),
            pltpu.VMEM((BLOCK, wide), f32),
            pltpu.VMEM((N_TP, 8, BLOCK), f32),
            pltpu.VMEM((BLOCK, HD), f32),
            pltpu.VMEM((N_TP, BLOCK, FEAT), bf),
            dma((3,)),
            dma((N_CTX,)), dma((N_CTX,)),
            dma((4, N_Y)), dma((4, N_Y)),
            dma((3, N_Y)), dma((3, N_Y)),
            dma((3, N_Y)), dma((3, N_Y)),
            dma((4, N_Y)), dma((4, N_Y)),
            dma((N_CTX,)), dma((N_CTX,)),
            dma((N_TP,)), dma((N_TP,)),
            dma((3,)), dma((3,)),
            dma((4,)), dma((4,)),
        ],
        cost_estimate=pl.CostEstimate(
            flops=60_000_000_000, bytes_accessed=200_000_000, transcendentals=3_000_000
        ),
        compiler_params=pltpu.CompilerParams(
            collective_id=3, has_side_effects=True, vmem_limit_bytes=56 * 2**20
        ),
    )(slots, pick, score, hidden, gain, grad, down, gate, up, wg, wu)


def body(
    hidden_in,
    norm_gain,
    out_grad,
    router_score,
    expert_ids,
    gate_saved,
    up_saved,
    w_gate,
    w_up,
    w_down,
    w_out,
    queries,
    keys,
    values,
):
    tok_rows = out_grad.shape[0]
    pad = W_ROWS - tok_rows
    shared_part = jnp.concatenate(
        [w_out.T, jnp.pad(keys, ((0, pad), (0, 0))), jnp.pad(values, ((0, pad), (0, 0)))], axis=1
    )
    gathered = lax.all_gather(shared_part, "ctx", axis=0, tiled=True)

    chosen = expert_ids
    chosen_row = chosen.reshape(1, tok_rows)
    earlier = (
        jnp.arange(tok_rows, dtype=jnp.int32)[None, :] < jnp.arange(tok_rows, dtype=jnp.int32)[:, None]
    )
    ranked = jnp.sum(((chosen == chosen_row) & earlier).astype(jnp.int32), axis=1)
    chosen = chosen[:, 0]
    slot_index = chosen * CAP + ranked
    placing = (
        jnp.arange(EXPERTS * CAP, dtype=jnp.int32)[:, None] == slot_index[None, :]
    ).astype(jnp.bfloat16)
    grad_slots = mm(placing, out_grad).astype(jnp.bfloat16).reshape(EXPERTS, CAP, FEAT)
    column = jnp.arange(N_Y * N_Z * CAP_PAD, dtype=jnp.int32)
    within = column % (N_Z * CAP_PAD)
    member = column // (N_Z * CAP_PAD) * N_Z + within // CAP
    column_slot = jnp.where(within < CHUNK, member // GROUP * CAP + within % CAP, -1)
    pick = (slot_index[:, None] == column_slot[None, :]).astype(jnp.bfloat16)
    d_hidden, stats, full_grad = expert_block(
        grad_slots,
        pick,
        router_score.astype(jnp.float32)[:, None],
        hidden_in,
        norm_gain[None, :],
        out_grad,
        w_down[0],
        gate_saved[0],
        up_saved[0],
        w_gate[0],
        w_up[0],
    )
    router_grad = stats[0]
    query_grad, key_grad, value_grad = attention(full_grad, queries, gathered)
    return (
        d_hidden,
        router_grad,
        query_grad,
        key_grad,
        value_grad,
    )


def solution(mesh):
    in_specs = (
        P("ctx", "tp"),
        P("tp"),
        P("ctx", "tp"),
        P("ctx"),
        P("ctx", None),
        P("ctx", "tp", None),
        P("ctx", "tp", None),
        P("ctx", "tp", None),
        P("ctx", "tp", None),
        P("ctx", None, "tp"),
        P("tp", "ctx"),
        P("ctx", "tp"),
        P("ctx", "tp"),
        P("ctx", "tp"),
    )
    out_specs = (P("ctx", "tp"), P("ctx"), P("ctx", "tp"), P("ctx", "tp"), P("ctx", "tp"))
    return jax.shard_map(body, mesh=mesh, in_specs=in_specs, out_specs=out_specs, check_vma=False)
```

```python
import jax
import jax.numpy as jnp
from jax import lax
from jax.experimental import pallas as pl
from jax.experimental.pallas import tpu as pltpu
from jax.sharding import PartitionSpec as P

D = 5120
QH = 40
KVH = 8
HD = 128
EXPERTS = 8
GROUP_Q = QH // KVH
N_CTX = 32
BLOCK = 128
PAIR = 2 * BLOCK
ROWS_Q = GROUP_Q * BLOCK
W_ROWS = 160
N_Y, N_Z, N_X, N_TP = 4, 8, 4, 8
GROUP = N_CTX // EXPERTS
CAP = 24
CAP_PAD = 32
CHUNK = N_Z * CAP
SLOTS = N_CTX * CAP
FEAT = D // N_TP
FF_GRP = 2048
FF_DEV = FF_GRP // N_TP
ROW_ORDER = (0, 1, 3, 2)
MESH = pl.DeviceIdType.MESH
EPSILON = 1e-05
NEG = -1e30
LOG2E = 1.4426950408889634


def silu_parts(gate_pre):
    sigmoid_val = jax.nn.sigmoid(gate_pre)
    return (gate_pre * sigmoid_val, sigmoid_val * (1.0 + gate_pre * (1.0 - sigmoid_val)))


def mm(a, b):
    return jnp.dot(a, b, preferred_element_type=jnp.float32)


def attention_kernel(
    full_ref, q5_ref, qt_ref, gathered_ref, dq_ref, dk_ref, dv_ref,
    w_buf, k_buf, v_buf, kt_buf, dt_buf, d5_buf, s_buf, dp_buf, p16_buf, ds16_buf,
    m_buf, l_buf, r_buf, f_buf, delta_buf, stat_buf, part_buf, dqt_buf, dk_acc, dv_acc,
    dq_send, dq_recv, kv_send, kv_recv,
    w_sem, kv_sem, d_send, d_recv, st_send, st_recv, pt_send, pt_recv,
    q_send, q_recv, o_send, o_recv,
):
    me = lax.axis_index("ctx")
    tp = lax.axis_index("tp")
    y, z = me // N_Z, me % N_Z
    scale = HD ** -0.5
    factor = scale * LOG2E

    def line(i):
        return ((y + i) % N_Y) * N_Z + z

    def pair_of(yk):
        return (yk - y + N_Y) % N_Y

    def remote(src, dst, send, recv, ctx):
        return pltpu.make_async_remote_copy(
            src_ref=src, dst_ref=dst, send_sem=send, recv_sem=recv,
            device_id=(ctx, tp), device_id_type=MESH,
        )

    source_row = (y - z // 2 + N_Y) % N_Y
    barrier = pltpu.get_barrier_semaphore()
    for i in range(1, N_Y):
        pl.semaphore_signal(barrier, inc=1, device_id=(line(i), tp), device_id_type=MESH)
    for i in range(N_Z):
        peer = source_row * N_Z + i

        @pl.when(peer != me)
        def _():
            pl.semaphore_signal(barrier, inc=1, device_id=(peer, tp), device_id_type=MESH)

    w_copy = pltpu.make_async_copy(gathered_ref.at[:, pl.ds(0, ROWS_Q)], w_buf, w_sem)
    kv_copies = []
    for yk in range(N_Y):
        for h in range(2):
            block = yk * N_Z + 2 * pair_of(yk) + h
            rows = pl.ds(pl.multiple_of(block * W_ROWS, W_ROWS), BLOCK)
            own = pl.ds(h * BLOCK, BLOCK)
            kv_copies += [
                pltpu.make_async_copy(
                    gathered_ref.at[rows, pl.ds(ROWS_Q, HD)], k_buf.at[yk, own], kv_sem.at[0, yk, h]
                ),
                pltpu.make_async_copy(
                    gathered_ref.at[rows, pl.ds(ROWS_Q + HD, HD)], v_buf.at[yk, own], kv_sem.at[1, yk, h]
                ),
            ]
    w_copy.start()
    for copy in kv_copies:
        copy.start()
    m_buf[...] = jnp.full(m_buf.shape, NEG, jnp.float32)
    for ref in (l_buf, r_buf, dqt_buf, dk_acc, dv_acc):
        ref[...] = jnp.zeros_like(ref)
    pl.semaphore_wait(barrier, N_Y - 1 + N_Z - jnp.where(z < 2, 1, 0))

    w_copy.wait()
    dout = mm(full_ref[0], w_buf[0:FEAT, :])
    for t in range(1, N_TP):
        dout = dout + mm(full_ref[t], w_buf[t * FEAT : (t + 1) * FEAT, :])
    dout = dout.astype(jnp.bfloat16)
    for h in range(GROUP_Q):
        rows = slice(h * BLOCK, (h + 1) * BLOCK)
        d5_buf[y, rows, :] = dout[:, rows]

    def d_copy(i, owner):
        return remote(d5_buf.at[owner], d5_buf.at[owner], d_send.at[i], d_recv.at[owner], line(i))

    for i in range(1, N_Y):
        d_copy(i, y).start()

    for copy in kv_copies:
        copy.wait()
    for yk in range(N_Y):
        kt_buf[yk] = k_buf[yk].astype(jnp.float32).T.astype(jnp.bfloat16)

    def fold(x, op):
        total = x[0:8]
        for i in range(1, x.shape[0] // 8):
            total = op(total, x[8 * i : 8 * i + 8])
        return total

    def partly(yk, step):
        @pl.when(2 * pair_of(yk) <= z)
        def _():
            step()

    step_rows = 32
    chunks = [slice(i * step_rows, (i + 1) * step_rows) for i in range(PAIR // step_rows)]

    def scores(yq, yk, masked):
        u = yq * N_Y + yk
        s_buf[u] = mm(k_buf[yk], qt_ref[yq])
        top = m_buf[yq]
        for rows in chunks:
            part = s_buf[u, rows, :]
            if masked:
                shape = (step_rows, ROWS_Q)
                key_pos = lax.broadcasted_iota(jnp.int32, shape, 0) + rows.start
                row_pos = lax.broadcasted_iota(jnp.int32, shape, 1) % BLOCK
                part = jnp.where(key_pos <= row_pos + (z - 2 * pair_of(yk)) * BLOCK, part, NEG)
                s_buf[u, rows, :] = part
            top = jnp.maximum(top, fold(part, jnp.maximum))
        m_buf[yq] = top

    def exponents(yq, yk):
        u = yq * N_Y + yk
        top = stat_buf[y, pl.ds(yq, 1), :]
        total = l_buf[yq]
        for rows in chunks:
            e = jnp.exp2((s_buf[u, rows, :] - top) * factor)
            s_buf[u, rows, :] = e
            total = total + fold(e, jnp.add)
        l_buf[yq] = total

    def each_query(yq, full_step, own_step):
        def step(yk, carry):
            full_step(yk)
            return carry

        lax.fori_loop(0, yq, step, 0)
        partly(yq, own_step)

    def score_row(yq, carry):
        each_query(yq, lambda yk: scores(yq, yk, False), lambda: scores(yq, yq, True))
        return carry

    lax.fori_loop(0, N_Y, score_row, 0)
    for yq in range(N_Y):
        stat_buf[y, yq : yq + 1, :] = jnp.max(m_buf[yq], axis=0, keepdims=True)

    def exponent_row(yq, carry):
        each_query(yq, lambda yk: exponents(yq, yk), lambda: exponents(yq, yq))
        return carry

    lax.fori_loop(0, N_Y, exponent_row, 0)
    for yq in range(N_Y):
        stat_buf[y, N_Y + yq : N_Y + yq + 1, :] = jnp.sum(l_buf[yq], axis=0, keepdims=True)

    def st_copy(i, owner):
        return remote(
            stat_buf.at[owner], stat_buf.at[owner], st_send.at[i], st_recv.at[owner], line(i)
        )

    for i in range(1, N_Y):
        st_copy(i, y).start()

    def prob_grads(yq, yk):
        u = yq * N_Y + yk
        dp_buf[u] = mm(v_buf[yk], dt_buf[yq])
        total = r_buf[yq]
        for rows in chunks:
            total = total + fold(s_buf[u, rows, :] * dp_buf[u, rows, :], jnp.add)
        r_buf[yq] = total

    def prob_row(i, carry):
        yq = (y + i) % N_Y

        @pl.when(i > 0)
        def _():
            d_copy(i, yq).wait_recv()

        for h in range(GROUP_Q):
            rows = slice(h * BLOCK, (h + 1) * BLOCK)
            dt_buf[yq, :, rows] = d5_buf[yq, rows, :].astype(jnp.float32).T.astype(jnp.bfloat16)
        each_query(yq, lambda yk: prob_grads(yq, yk), lambda: prob_grads(yq, yq))
        return carry

    lax.fori_loop(0, N_Y, prob_row, 0)

    for i in range(1, N_Y):
        st_copy(i, (y + i) % N_Y).wait_recv()
    top_all = stat_buf[0, 0:N_Y, :]
    for t in range(1, N_Y):
        top_all = jnp.maximum(top_all, stat_buf[t, 0:N_Y, :])
    sum_all = jnp.zeros_like(top_all)
    for t in range(N_Y):
        sum_all = sum_all + stat_buf[t, N_Y : 2 * N_Y, :] * jnp.exp2(
            (stat_buf[t, 0:N_Y, :] - top_all) * factor
        )
    share = jnp.exp2((stat_buf[y, 0:N_Y, :] - top_all) * factor) / sum_all
    f_buf[0:N_Y, :] = share
    part_buf[y] = jnp.zeros((8, ROWS_Q), jnp.float32)
    for yq in range(N_Y):
        part_buf[y, yq : yq + 1, :] = (
            jnp.sum(r_buf[yq], axis=0, keepdims=True) * share[yq : yq + 1, :]
        )

    def pt_copy(i, owner):
        return remote(
            part_buf.at[owner], part_buf.at[owner], pt_send.at[i], pt_recv.at[owner], line(i)
        )

    for i in range(1, N_Y):
        pt_copy(i, y).start()

    def block_copy(which, yk, h):
        return remote(
            kv_send.at[which, 2 * yk + h],
            kv_recv.at[which, z],
            o_send.at[which, 2 * yk + h],
            o_recv.at[which, z],
            yk * N_Z + 2 * pair_of(yk) + h,
        )

    def give(which, yk, acc):
        for h in range(2):
            kv_send[which, 2 * yk + h] = acc[h * BLOCK : (h + 1) * BLOCK].astype(jnp.bfloat16)
            owner = yk * N_Z + 2 * pair_of(yk) + h

            @pl.when(owner != me)
            def _():
                block_copy(which, yk, h).start()

            @pl.when(owner == me)
            def _():
                kv_recv[which, z] = kv_send[which, 2 * yk + h]

    def value_grads(yq, yk):
        u = yq * N_Y + yk
        share_row = f_buf[pl.ds(yq, 1), :]
        for rows in chunks:
            prob = s_buf[u, rows, :] * share_row
            s_buf[u, rows, :] = prob
            p16_buf[rows, :] = prob.astype(jnp.bfloat16)
        dv_acc[yk] += mm(p16_buf[...], d5_buf[yq])

    def each_key(yk, full_step, own_step):
        def step(yq, carry):
            full_step(yq)
            return carry

        partly(yk, own_step)
        lax.fori_loop(yk + 1, N_Y, step, 0)

    def value_row(yk, carry):
        each_key(yk, lambda yq: value_grads(yq, yk), lambda: value_grads(yk, yk))
        give(0, yk, dv_acc[yk])
        return carry

    lax.fori_loop(0, N_Y, value_row, 0)

    for i in range(1, N_Y):
        pt_copy(i, (y + i) % N_Y).wait_recv()
    delta_buf[...] = part_buf[0] + part_buf[1] + part_buf[2] + part_buf[3]

    def key_grads(yq, yk):
        u = yq * N_Y + yk
        delta = delta_buf[pl.ds(yq, 1), :]
        for rows in chunks:
            ds16_buf[rows, :] = (
                s_buf[u, rows, :] * (dp_buf[u, rows, :] - delta)
            ).astype(jnp.bfloat16)
        ds16 = ds16_buf[...]
        dk_acc[yk] += mm(ds16, q5_ref[yq])
        dqt_buf[yq] += mm(kt_buf[yk], ds16)

    def dq_copy(yq):
        return remote(
            dq_send.at[yq], dq_recv.at[y], q_send.at[yq], q_recv.at[y], yq * N_Z + z
        )

    def key_row(yk, carry):
        each_key(yk, lambda yq: key_grads(yq, yk), lambda: key_grads(yk, yk))
        give(1, yk, dk_acc[yk] * scale)
        dq_send[yk] = (dqt_buf[yk] * scale).astype(jnp.bfloat16)

        @pl.when(yk != y)
        def _():
            dq_copy(yk).start()

        return carry

    lax.fori_loop(0, N_Y, key_row, 0)

    total = dq_send[y].astype(jnp.float32)
    for i in range(1, N_Y):
        peer = (y + i) % N_Y
        remote(
            dq_send.at[y], dq_recv.at[peer], q_send.at[y], q_recv.at[peer], line(i)
        ).wait_recv()
        total = total + dq_recv[peer].astype(jnp.float32)
    for h in range(GROUP_Q):
        cols = slice(h * BLOCK, (h + 1) * BLOCK)
        dq_ref[:, cols] = total[:, cols].T.astype(jnp.bfloat16)

    for which, out_ref in ((0, dv_ref), (1, dk_ref)):
        total = jnp.zeros((BLOCK, HD), jnp.float32)
        for i in range(N_Z):
            peer = source_row * N_Z + i

            @pl.when(peer != me)
            def _():
                remote(
                    kv_send.at[which, 0], kv_recv.at[which, i], o_send.at[which, 0],
                    o_recv.at[which, i], peer,
                ).wait_recv()

            total = total + kv_recv[which, i].astype(jnp.float32)
        out_ref[...] = total.astype(jnp.bfloat16)

    for i in range(1, N_Y):
        d_copy(i, y).wait_send()
        st_copy(i, y).wait_send()
        pt_copy(i, y).wait_send()
        dq_copy((y + i) % N_Y).wait_send()
    for which in range(2):
        for yk in range(N_Y):
            for h in range(2):

                @pl.when(yk * N_Z + 2 * pair_of(yk) + h != me)
                def _():
                    block_copy(which, yk, h).wait_send()


def attention(full_grad, q5, qt, gathered):
    bf, f32 = jnp.bfloat16, jnp.float32
    vmem = pl.BlockSpec(memory_space=pltpu.VMEM)
    dma = pltpu.SemaphoreType.DMA
    units = N_Y * N_Y
    return pl.pallas_call(
        attention_kernel,
        name="attention_grads",
        out_shape=[
            jax.ShapeDtypeStruct((BLOCK, ROWS_Q), bf),
            jax.ShapeDtypeStruct((BLOCK, HD), bf),
            jax.ShapeDtypeStruct((BLOCK, HD), bf),
        ],
        in_specs=[vmem, vmem, vmem, pl.BlockSpec(memory_space=pl.ANY)],
        out_specs=[vmem, vmem, vmem],
        scratch_shapes=[
            pltpu.VMEM((D, ROWS_Q), bf),
            pltpu.VMEM((N_Y, PAIR, HD), bf),
            pltpu.VMEM((N_Y, PAIR, HD), bf),
            pltpu.VMEM((N_Y, HD, PAIR), bf),
            pltpu.VMEM((N_Y, HD, ROWS_Q), bf),
            pltpu.VMEM((N_Y, ROWS_Q, HD), bf),
            pltpu.VMEM((units, PAIR, ROWS_Q), f32),
            pltpu.VMEM((units, PAIR, ROWS_Q), f32),
            pltpu.VMEM((PAIR, ROWS_Q), bf),
            pltpu.VMEM((PAIR, ROWS_Q), bf),
            pltpu.VMEM((N_Y, 8, ROWS_Q), f32),
            pltpu.VMEM((N_Y, 8, ROWS_Q), f32),
            pltpu.VMEM((N_Y, 8, ROWS_Q), f32),
            pltpu.VMEM((8, ROWS_Q), f32),
            pltpu.VMEM((8, ROWS_Q), f32),
            pltpu.VMEM((N_Y, 8, ROWS_Q), f32),
            pltpu.VMEM((N_Y, 8, ROWS_Q), f32),
            pltpu.VMEM((N_Y, HD, ROWS_Q), f32),
            pltpu.VMEM((N_Y, PAIR, HD), f32),
            pltpu.VMEM((N_Y, PAIR, HD), f32),
            pltpu.VMEM((N_Y, HD, ROWS_Q), bf),
            pltpu.VMEM((N_Y, HD, ROWS_Q), bf),
            pltpu.VMEM((2, 2 * N_Y, BLOCK, HD), bf),
            pltpu.VMEM((2, N_Z, BLOCK, HD), bf),
            dma,
            dma((2, N_Y, 2)),
            dma((N_Y,)), dma((N_Y,)),
            dma((N_Y,)), dma((N_Y,)),
            dma((N_Y,)), dma((N_Y,)),
            dma((N_Y,)), dma((N_Y,)),
            dma((2, 2 * N_Y)), dma((2, N_Z)),
        ],
        cost_estimate=pl.CostEstimate(
            flops=6_000_000_000, bytes_accessed=12_000_000, transcendentals=3_000_000
        ),
        compiler_params=pltpu.CompilerParams(
            collective_id=4, has_side_effects=True, vmem_limit_bytes=56 * 2**20
        ),
    )(full_grad, q5, qt, gathered)


def dot_nt(a, b):
    return lax.dot_general(a, b, (((1,), (1,)), ((), ())), preferred_element_type=jnp.float32)


def expert_kernel(
    slots_ref, pick_ref, score_ref, hidden_ref, gain_ref, grad_ref, q_ref,
    down_ref, gate_ref, up_ref, wg_ref, wu_ref,
    dh_ref, stat_ref, full_ref, q5_ref, qt_ref,
    down, wg, wu, recv_d, flat, slots, own, sib_out, sib_in, x_out, x_in,
    act_buf, slope_buf, prod_buf, ag, acc, back, ret, picked, stats, square, full, q5,
    w_sem, d_send, d_recv, s_send, s_recv, x_send, x_recv, ax_send, ax_recv,
    as_send, as_recv, b_send, b_recv, t_send, t_recv, fx_send, fx_recv, fs_send, fs_recv, q_send, q_recv,
):
    me = lax.axis_index("ctx")
    tp = lax.axis_index("tp")
    y, z = me // N_Z, me % N_Z
    x, k = tp // 2, tp % 2
    sibling = 2 * x + (1 - k)
    far = (2, 1, 3)

    def chip(dx):
        return (x + dx) % N_X

    def remote(src, dst, send, recv, ctx, peer):
        return pltpu.make_async_remote_copy(
            src_ref=src, dst_ref=dst, send_sem=send, recv_sem=recv,
            device_id=(ctx, peer), device_id_type=MESH,
        )

    w_copies = [
        pltpu.make_async_copy(down_ref, down, w_sem.at[0]),
        pltpu.make_async_copy(wg_ref, wg, w_sem.at[1]),
        pltpu.make_async_copy(wu_ref, wu, w_sem.at[2]),
    ]
    for copy in w_copies:
        copy.start()

    barrier = pltpu.get_barrier_semaphore()

    def greet_ctx(i, carry):
        pl.semaphore_signal(
            barrier, inc=1, device_id=((me + i) % N_CTX, tp), device_id_type=MESH
        )
        return carry

    def greet_tp(i, carry):
        pl.semaphore_signal(
            barrier, inc=1, device_id=(me, (tp + i) % N_TP), device_id_type=MESH
        )
        return carry

    lax.fori_loop(1, N_CTX, greet_ctx, 0)
    lax.fori_loop(1, N_TP, greet_tp, 0)
    hidden_val = hidden_ref[...].astype(jnp.float32)
    square[...] = jnp.broadcast_to(
        jnp.sum(hidden_val * hidden_val, axis=1, keepdims=True), square.shape
    )
    pl.semaphore_wait(barrier, N_CTX - 1 + N_TP - 1)

    def dispatch(j):
        return remote(
            slots_ref.at[j // GROUP], recv_d.at[me], d_send.at[j], d_recv.at[me], j, tp
        )

    for dy in ROW_ORDER:
        row = (y - dy + N_Y) % N_Y

        def send_step(dz, carry, row=row):
            dispatch(row * N_Z + (z + dz) % N_Z).start()
            return carry

        lax.fori_loop(1 if dy == 0 else 0, N_Z, send_step, 0)
    recv_d[me] = slots_ref[me // GROUP]

    def q_copy(i, owner):
        ctx = ((y + i) % N_Y) * N_Z + z
        return remote(q5.at[owner], q5.at[owner], q_send.at[i], q_recv.at[owner], ctx, tp)

    for h in range(GROUP_Q):
        heads = slice(h * BLOCK, (h + 1) * BLOCK)
        q5[y, heads, :] = q_ref[:, heads]
    for i in range(1, N_Y):
        q_copy(i, y).start()

    def turn_queries():
        for i in range(1, N_Y):
            q_copy(i, (y + i) % N_Y).wait_recv()
        q5_ref[...] = q5[...]
        for r in range(N_Y):
            for h in range(GROUP_Q):
                heads = slice(h * BLOCK, (h + 1) * BLOCK)
                qt_ref[r, :, heads] = q5[r, heads, :].astype(jnp.float32).T.astype(jnp.bfloat16)

    def chunk_rows(ch):
        start = ((y + ROW_ORDER[ch]) % N_Y) * CHUNK
        return pl.ds(pl.multiple_of(start, CHUNK), CHUNK)

    def arrive(ch):
        first = ((y + ROW_ORDER[ch]) % N_Y) * N_Z
        for i in range(N_Z):
            j = first + i

            @pl.when(j != me)
            def _():
                remote(
                    slots_ref.at[0], recv_d.at[j], d_send.at[j], d_recv.at[j], j, tp
                ).wait_recv()

            flat[i * CAP : (i + 1) * CAP, :] = recv_d[j].astype(jnp.float32)
        slots[chunk_rows(ch), :] = flat[...].astype(jnp.bfloat16)

    def sib_copy(i, ch):
        rows = chunk_rows(ch)
        return remote(
            sib_out.at[i, rows], sib_in.at[i, rows], s_send.at[i, ch], s_recv.at[i, ch],
            me, sibling,
        )

    def x_copy(i, ch):
        rows = chunk_rows(ch)
        return remote(
            x_out.at[i, rows], x_in.at[i, rows], x_send.at[i, ch], x_recv.at[i, ch],
            me, 2 * chip(far[i]) + k,
        )

    def stage1(ch):
        rows = chunk_rows(ch)
        part = slots[rows, :]
        for i, dx in enumerate(far + (0,)):
            base = 2 * chip(dx)

            def block(t):
                start = pl.multiple_of(t * FF_DEV, FF_DEV)
                return dot_nt(part, down[pl.ds(start, FF_DEV), :]).astype(jnp.bfloat16)

            sib_out[i, rows, :] = block(base + 1 - k)
            sib_copy(i, ch).start()
            own[i, rows, :] = block(base + k)

    def joined(i, ch):
        rows = chunk_rows(ch)
        sib_copy(i, ch).wait_recv()
        return own[i, rows, :].astype(jnp.float32) + sib_in[i, rows, :].astype(jnp.float32)

    def stage2(ch):
        rows = chunk_rows(ch)
        for i in range(3):
            x_out[i, rows, :] = joined(i, ch).astype(jnp.bfloat16)
            x_copy(i, ch).start()

    def prepare():
        gate = gate_ref[...].astype(jnp.float32).T
        up = up_ref[...].astype(jnp.float32).T
        act, slope = silu_parts(gate)
        act_buf[...] = act
        slope_buf[...] = up * slope
        prod_buf[...] = act * up

    def ag_out(i, ch):
        rows = chunk_rows(ch)
        return remote(
            ag.at[tp, rows], ag.at[tp, rows], ax_send.at[i, ch], ax_recv.at[i, ch],
            me, 2 * chip(far[i]) + k,
        )

    def ag_chip(i, ch):
        return 2 * chip(N_X - far[i]) + k

    def ag_in(i, ch):
        rows = chunk_rows(ch)
        t = ag_chip(i, ch)
        return remote(
            ag.at[t, rows], ag.at[t, rows], ax_send.at[i, ch], ax_recv.at[i, ch], me, t
        )

    def ag_share(t, i, ch):
        rows = chunk_rows(ch)
        return remote(
            ag.at[t, rows], ag.at[t, rows], as_send.at[i, ch], as_recv.at[i, ch], me, sibling
        )

    def stage3(ch):
        rows = chunk_rows(ch)
        hid = joined(3, ch)
        for i in range(3):
            x_copy(i, ch).wait_recv()
            hid = hid + x_in[i, rows, :].astype(jnp.float32)
        ag[tp, rows, 0:FF_DEV] = (hid * slope_buf[rows, :]).astype(jnp.bfloat16)
        ag[tp, rows, FF_DEV : 2 * FF_DEV] = (hid * act_buf[rows, :]).astype(jnp.bfloat16)
        for i in range(3):
            ag_out(i, ch).start()
        ag_share(tp, 3, ch).start()
        term = jnp.sum(hid * prod_buf[rows, :], axis=1, keepdims=True)
        prod_buf[rows, 0:HD] = jnp.broadcast_to(term, (CHUNK, HD))

    def product(t, rows):
        cols = pl.ds(pl.multiple_of(t * FF_DEV, FF_DEV), FF_DEV)
        return dot_nt(ag[t, rows, 0:FF_DEV], wg[:, cols]) + dot_nt(
            ag[t, rows, FF_DEV : 2 * FF_DEV], wu[:, cols]
        )

    def back_copy(j):
        return remote(back.at[j], ret.at[me], b_send.at[j], b_recv.at[me], j, tp)

    def stage4(ch):
        rows = chunk_rows(ch)
        acc[:, FEAT : FEAT + HD] = prod_buf[rows, 0:HD]
        acc[:, 0:FEAT] = product(tp, rows)
        for i in (1, 2, 0):
            ag_in(i, ch).wait_recv()
            ag_share(ag_chip(i, ch), i, ch).start()
            acc[:, 0:FEAT] += product(ag_chip(i, ch), rows)
        for i in (3, 1, 2, 0):
            t = sibling if i == 3 else ag_chip(i, ch) + 1 - 2 * k
            ag_share(t, i, ch).wait_recv()
            acc[:, 0:FEAT] += product(t, rows)
        first = ((y + ROW_ORDER[ch]) % N_Y) * N_Z
        for i in range(N_Z):
            j = first + i
            back[j] = acc[i * CAP : (i + 1) * CAP, :].astype(jnp.bfloat16)

            @pl.when(j != me)
            def _():
                back_copy(j).start()

    w_copies[0].wait()
    arrive(0)
    stage1(0)
    arrive(1)
    stage1(1)
    stage2(0)
    arrive(2)
    stage1(2)
    stage2(1)
    arrive(3)
    stage1(3)
    stage2(2)
    stage2(3)
    prepare()
    turn_queries()
    w_copies[1].wait()
    w_copies[2].wait()
    for ch in range(N_Y):
        stage3(ch)
    for ch in range(N_Y):
        stage4(ch)
    ret[me] = back[me]

    picked[...] = jnp.zeros_like(picked)
    for ch in range(N_Y):
        first = ((y - ROW_ORDER[ch] + N_Y) % N_Y) * N_Z
        for i in range(N_Z):
            j = first + i

            @pl.when(j != me)
            def _():
                remote(back.at[j], ret.at[j], b_send.at[j], b_recv.at[j], j, tp).wait_recv()

            acc[i * CAP : (i + 1) * CAP, :] = ret[j].astype(jnp.float32)
        cols = pl.ds(pl.multiple_of(first * CAP_PAD, N_Z * CAP_PAD), N_Z * CAP_PAD)
        picked[...] += mm(pick_ref[:, cols][:, 0:CHUNK], acc[...].astype(jnp.bfloat16))

    norm_grad = picked[:, 0:FEAT] * score_ref[...]
    hidden_now = hidden_ref[...].astype(jnp.float32)
    gain_val = gain_ref[...].astype(jnp.float32)
    cross = jnp.sum(hidden_now * gain_val * norm_grad, axis=1, keepdims=True)
    lane = lax.broadcasted_iota(jnp.int32, (BLOCK, HD), 1)
    packed = jnp.where(
        lane == 0, picked[:, FEAT : FEAT + HD], jnp.where(lane == 1, square[...], cross)
    )
    stats[tp] = packed.T[0:8, :]

    def stat_copy(peer, src):
        return remote(
            stats.at[src], stats.at[src], t_send.at[peer], t_recv.at[src], me, peer
        )

    def stat_start(i, carry):
        stat_copy((tp + i) % N_TP, tp).start()
        return carry

    def stat_wait(i, carry):
        stat_copy((tp + i) % N_TP, (tp + i) % N_TP).wait_recv()
        return carry

    lax.fori_loop(1, N_TP, stat_start, 0)
    lax.fori_loop(1, N_TP, stat_wait, 0)
    total = stats[0]
    for t in range(1, N_TP):
        total = total + stats[t]
    stat_ref[...] = total
    spread = jnp.concatenate([total] * (BLOCK // 8), axis=0).T
    inverse_rms = lax.rsqrt(spread[:, 1:2] / D + EPSILON)
    cross_sum = spread[:, 2:3]
    d_hidden = (
        grad_ref[...].astype(jnp.float32)
        + inverse_rms * gain_val * norm_grad
        - hidden_now * inverse_rms * inverse_rms * inverse_rms * cross_sum / D
    ).astype(jnp.bfloat16)
    dh_ref[...] = d_hidden
    full[tp] = d_hidden

    def full_out(i):
        return remote(
            full.at[tp], full.at[tp], fx_send.at[i], fx_recv.at[i], me, 2 * chip(far[i]) + k
        )

    def full_in(i):
        t = ag_chip(i, 0)
        return remote(full.at[t], full.at[t], fx_send.at[i], fx_recv.at[i], me, t)

    def full_share(t, i):
        return remote(full.at[t], full.at[t], fs_send.at[i], fs_recv.at[i], me, sibling)

    for i in range(3):
        full_out(i).start()
    full_share(tp, 3).start()
    for i in (1, 2, 0):
        full_in(i).wait_recv()
        full_share(ag_chip(i, 0), i).start()
    for i in (3, 1, 2, 0):
        t = sibling if i == 3 else ag_chip(i, 0) + 1 - 2 * k
        full_share(t, i).wait_recv()
    full_ref[...] = full[...]

    def drain_ctx(i, carry):
        j = (me + i) % N_CTX
        dispatch(j).wait_send()
        back_copy(j).wait_send()
        return carry

    def drain_tp(i, carry):
        stat_copy((tp + i) % N_TP, tp).wait_send()
        return carry

    lax.fori_loop(1, N_CTX, drain_ctx, 0)
    lax.fori_loop(1, N_TP, drain_tp, 0)
    for ch in range(N_Y):
        for i in range(4):
            sib_copy(i, ch).wait_send()
            ag_share(tp, i, ch).wait_send()
        for i in range(3):
            x_copy(i, ch).wait_send()
            ag_out(i, ch).wait_send()
    for i in range(1, N_Y):
        q_copy(i, y).wait_send()
    for i in range(3):
        full_out(i).wait_send()
    for i in range(4):
        full_share(tp, i).wait_send()


def expert_block(slots, pick, score, hidden, gain, grad, queries, down, gate, up, wg, wu):
    bf, f32 = jnp.bfloat16, jnp.float32
    vmem = pl.BlockSpec(memory_space=pltpu.VMEM)
    hbm = pl.BlockSpec(memory_space=pl.ANY)
    dma = pltpu.SemaphoreType.DMA
    wide = FEAT + HD
    return pl.pallas_call(
        expert_kernel,
        name="expert_block",
        out_shape=[
            jax.ShapeDtypeStruct((BLOCK, FEAT), bf),
            jax.ShapeDtypeStruct((8, BLOCK), f32),
            jax.ShapeDtypeStruct((N_TP, BLOCK, FEAT), bf),
            jax.ShapeDtypeStruct((N_Y, ROWS_Q, HD), bf),
            jax.ShapeDtypeStruct((N_Y, HD, ROWS_Q), bf),
        ],
        in_specs=[vmem] * 7 + [hbm, vmem, vmem, hbm, hbm],
        out_specs=[vmem] * 5,
        scratch_shapes=[
            pltpu.VMEM((FF_GRP, FEAT), bf),
            pltpu.VMEM((FEAT, FF_GRP), bf),
            pltpu.VMEM((FEAT, FF_GRP), bf),
            pltpu.VMEM((N_CTX, CAP, FEAT), bf),
            pltpu.VMEM((CHUNK, FEAT), f32),
            pltpu.VMEM((SLOTS, FEAT), bf),
            pltpu.VMEM((4, SLOTS, FF_DEV), bf),
            pltpu.VMEM((4, SLOTS, FF_DEV), bf),
            pltpu.VMEM((4, SLOTS, FF_DEV), bf),
            pltpu.VMEM((3, SLOTS, FF_DEV), bf),
            pltpu.VMEM((3, SLOTS, FF_DEV), bf),
            pltpu.VMEM((SLOTS, FF_DEV), f32),
            pltpu.VMEM((SLOTS, FF_DEV), f32),
            pltpu.VMEM((SLOTS, FF_DEV), f32),
            pltpu.VMEM((N_TP, SLOTS, 2 * FF_DEV), bf),
            pltpu.VMEM((CHUNK, wide), f32),
            pltpu.VMEM((N_CTX, CAP, wide), bf),
            pltpu.VMEM((N_CTX, CAP, wide), bf),
            pltpu.VMEM((BLOCK, wide), f32),
            pltpu.VMEM((N_TP, 8, BLOCK), f32),
            pltpu.VMEM((BLOCK, HD), f32),
            pltpu.VMEM((N_TP, BLOCK, FEAT), bf),
            pltpu.VMEM((N_Y, ROWS_Q, HD), bf),
            dma((3,)),
            dma((N_CTX,)), dma((N_CTX,)),
            dma((4, N_Y)), dma((4, N_Y)),
            dma((3, N_Y)), dma((3, N_Y)),
            dma((3, N_Y)), dma((3, N_Y)),
            dma((4, N_Y)), dma((4, N_Y)),
            dma((N_CTX,)), dma((N_CTX,)),
            dma((N_TP,)), dma((N_TP,)),
            dma((3,)), dma((3,)),
            dma((4,)), dma((4,)),
            dma((N_Y,)), dma((N_Y,)),
        ],
        cost_estimate=pl.CostEstimate(
            flops=60_000_000_000, bytes_accessed=200_000_000, transcendentals=3_000_000
        ),
        compiler_params=pltpu.CompilerParams(
            collective_id=3, has_side_effects=True, vmem_limit_bytes=56 * 2**20
        ),
    )(slots, pick, score, hidden, gain, grad, queries, down, gate, up, wg, wu)


def body(
    hidden_in,
    norm_gain,
    out_grad,
    router_score,
    expert_ids,
    gate_saved,
    up_saved,
    w_gate,
    w_up,
    w_down,
    w_out,
    queries,
    keys,
    values,
):
    tok_rows = out_grad.shape[0]
    pad = W_ROWS - tok_rows
    shared_part = jnp.concatenate(
        [w_out.T, jnp.pad(keys, ((0, pad), (0, 0))), jnp.pad(values, ((0, pad), (0, 0)))], axis=1
    )
    gathered = lax.all_gather(shared_part, "ctx", axis=0, tiled=True)

    chosen = expert_ids
    chosen_row = chosen.reshape(1, tok_rows)
    earlier = (
        jnp.arange(tok_rows, dtype=jnp.int32)[None, :] < jnp.arange(tok_rows, dtype=jnp.int32)[:, None]
    )
    ranked = jnp.sum(((chosen == chosen_row) & earlier).astype(jnp.int32), axis=1)
    chosen = chosen[:, 0]
    slot_index = chosen * CAP + ranked
    placing = (
        jnp.arange(EXPERTS * CAP, dtype=jnp.int32)[:, None] == slot_index[None, :]
    ).astype(jnp.bfloat16)
    grad_slots = mm(placing, out_grad).astype(jnp.bfloat16).reshape(EXPERTS, CAP, FEAT)
    column = jnp.arange(N_Y * N_Z * CAP_PAD, dtype=jnp.int32)
    within = column % (N_Z * CAP_PAD)
    member = column // (N_Z * CAP_PAD) * N_Z + within // CAP
    column_slot = jnp.where(within < CHUNK, member // GROUP * CAP + within % CAP, -1)
    pick = (slot_index[:, None] == column_slot[None, :]).astype(jnp.bfloat16)
    d_hidden, stats, full_grad, q5, qt = expert_block(
        grad_slots,
        pick,
        router_score.astype(jnp.float32)[:, None],
        hidden_in,
        norm_gain[None, :],
        out_grad,
        queries,
        w_down[0],
        gate_saved[0],
        up_saved[0],
        w_gate[0],
        w_up[0],
    )
    router_grad = stats[0]
    query_grad, key_grad, value_grad = attention(full_grad, q5, qt, gathered)
    return (
        d_hidden,
        router_grad,
        query_grad,
        key_grad,
        value_grad,
    )


def solution(mesh):
    in_specs = (
        P("ctx", "tp"),
        P("tp"),
        P("ctx", "tp"),
        P("ctx"),
        P("ctx", None),
        P("ctx", "tp", None),
        P("ctx", "tp", None),
        P("ctx", "tp", None),
        P("ctx", "tp", None),
        P("ctx", None, "tp"),
        P("tp", "ctx"),
        P("ctx", "tp"),
        P("ctx", "tp"),
        P("ctx", "tp"),
    )
    out_specs = (P("ctx", "tp"), P("ctx"), P("ctx", "tp"), P("ctx", "tp"), P("ctx", "tp"))
    return jax.shard_map(body, mesh=mesh, in_specs=in_specs, out_specs=out_specs, check_vma=False)
```

```python
import jax
import jax.numpy as jnp
from jax import lax
from jax.experimental import pallas as pl
from jax.experimental.pallas import tpu as pltpu
from jax.sharding import PartitionSpec as P

D = 5120
QH = 40
KVH = 8
HD = 128
EXPERTS = 8
GROUP_Q = QH // KVH
N_CTX = 32
BLOCK = 128
PAIR = 2 * BLOCK
ROWS_Q = GROUP_Q * BLOCK
N_Y, N_Z, N_X, N_TP = 4, 8, 4, 8
GROUP = N_CTX // EXPERTS
CAP = 24
CAP_PAD = 32
CHUNK = N_Z * CAP
SLOTS = N_CTX * CAP
FEAT = D // N_TP
FF_GRP = 2048
FF_DEV = FF_GRP // N_TP
PAIR_ROWS = 2 * CHUNK
MESH = pl.DeviceIdType.MESH
EPSILON = 1e-05
NEG = -1e30
LOG2E = 1.4426950408889634


def silu_parts(gate_pre):
    sigmoid_val = jax.nn.sigmoid(gate_pre)
    return (gate_pre * sigmoid_val, sigmoid_val * (1.0 + gate_pre * (1.0 - sigmoid_val)))


def mm(a, b):
    return jnp.dot(a, b, preferred_element_type=jnp.float32)


def attention_kernel(
    full_ref, q5_ref, qt_ref, kv_ref, gathered_ref, out_ref,
    w_buf, k_buf, v_buf, kt_buf, dt_buf, d5_buf, s_buf, dp_buf, p16_buf, ds16_buf,
    m_buf, l_buf, r_buf, f_buf, delta_buf, stat_buf, part_buf, dqt_buf, dk_acc, dv_acc,
    dq_send, dq_recv, kv_send, kv_recv,
    w_sem, d_send, d_recv, st_send, st_recv, pt_send, pt_recv,
    q_send, q_recv, o_send, o_recv,
):
    me = lax.axis_index("ctx")
    tp = lax.axis_index("tp")
    y, z = me // N_Z, me % N_Z
    scale = HD ** -0.5
    factor = scale * LOG2E

    def line(i):
        return ((y + i) % N_Y) * N_Z + z

    def pair_of(yk):
        return (yk - y + N_Y) % N_Y

    def remote(src, dst, send, recv, ctx):
        return pltpu.make_async_remote_copy(
            src_ref=src, dst_ref=dst, send_sem=send, recv_sem=recv,
            device_id=(ctx, tp), device_id_type=MESH,
        )

    source_row = (y - z // 2 + N_Y) % N_Y
    barrier = pltpu.get_barrier_semaphore()
    for i in range(1, N_Y):
        pl.semaphore_signal(barrier, inc=1, device_id=(line(i), tp), device_id_type=MESH)
    for i in range(N_Z):
        peer = source_row * N_Z + i

        @pl.when(peer != me)
        def _():
            pl.semaphore_signal(barrier, inc=1, device_id=(peer, tp), device_id_type=MESH)

    w_copy = pltpu.make_async_copy(gathered_ref, w_buf, w_sem)
    w_copy.start()
    for yk in range(N_Y):
        for h in range(2):
            rows = slice(h * BLOCK, (h + 1) * BLOCK)
            k_buf[yk, rows, :] = kv_ref[yk, h, 0]
            v_buf[yk, rows, :] = kv_ref[yk, h, 1]
        kt_buf[yk] = k_buf[yk].astype(jnp.float32).T.astype(jnp.bfloat16)
    m_buf[...] = jnp.full(m_buf.shape, NEG, jnp.float32)
    for ref in (l_buf, r_buf, dqt_buf, dk_acc, dv_acc):
        ref[...] = jnp.zeros_like(ref)

    w_copy.wait()
    dout = mm(full_ref[0], w_buf[0:FEAT, :])
    for t in range(1, N_TP):
        dout = dout + mm(full_ref[t], w_buf[t * FEAT : (t + 1) * FEAT, :])
    dout = dout.astype(jnp.bfloat16)
    for h in range(GROUP_Q):
        rows = slice(h * BLOCK, (h + 1) * BLOCK)
        d5_buf[y, rows, :] = dout[:, rows]

    pl.semaphore_wait(barrier, N_Y - 1 + N_Z - jnp.where(z < 2, 1, 0))

    def d_copy(i, owner):
        return remote(d5_buf.at[owner], d5_buf.at[owner], d_send.at[i], d_recv.at[owner], line(i))

    for i in range(1, N_Y):
        d_copy(i, y).start()

    def fold(x, op):
        total = x[0:8]
        for i in range(1, x.shape[0] // 8):
            total = op(total, x[8 * i : 8 * i + 8])
        return total

    def partly(yk, step):
        @pl.when(2 * pair_of(yk) <= z)
        def _():
            step()

    step_rows = 32
    chunks = [slice(i * step_rows, (i + 1) * step_rows) for i in range(PAIR // step_rows)]

    def scores(yq, yk, masked):
        u = yq * N_Y + yk
        s_buf[u] = mm(k_buf[yk], qt_ref[yq])
        top = m_buf[yq]
        for rows in chunks:
            part = s_buf[u, rows, :]
            if masked:
                shape = (step_rows, ROWS_Q)
                key_pos = lax.broadcasted_iota(jnp.int32, shape, 0) + rows.start
                row_pos = lax.broadcasted_iota(jnp.int32, shape, 1) % BLOCK
                part = jnp.where(key_pos <= row_pos + (z - 2 * pair_of(yk)) * BLOCK, part, NEG)
                s_buf[u, rows, :] = part
            top = jnp.maximum(top, fold(part, jnp.maximum))
        m_buf[yq] = top

    def exponents(yq, yk):
        u = yq * N_Y + yk
        top = stat_buf[y, pl.ds(yq, 1), :]
        total = l_buf[yq]
        for rows in chunks:
            e = jnp.exp2((s_buf[u, rows, :] - top) * factor)
            s_buf[u, rows, :] = e
            total = total + fold(e, jnp.add)
        l_buf[yq] = total

    def each_query(yq, full_step, own_step):
        def step(yk, carry):
            full_step(yk)
            return carry

        lax.fori_loop(0, yq, step, 0)
        partly(yq, own_step)

    def score_row(yq, carry):
        each_query(yq, lambda yk: scores(yq, yk, False), lambda: scores(yq, yq, True))
        return carry

    lax.fori_loop(0, N_Y, score_row, 0)
    for yq in range(N_Y):
        stat_buf[y, yq : yq + 1, :] = jnp.max(m_buf[yq], axis=0, keepdims=True)

    def exponent_row(yq, carry):
        each_query(yq, lambda yk: exponents(yq, yk), lambda: exponents(yq, yq))
        return carry

    lax.fori_loop(0, N_Y, exponent_row, 0)
    for yq in range(N_Y):
        stat_buf[y, N_Y + yq : N_Y + yq + 1, :] = jnp.sum(l_buf[yq], axis=0, keepdims=True)

    def st_copy(i, owner):
        return remote(
            stat_buf.at[owner], stat_buf.at[owner], st_send.at[i], st_recv.at[owner], line(i)
        )

    for i in range(1, N_Y):
        st_copy(i, y).start()

    def prob_grads(yq, yk):
        u = yq * N_Y + yk
        dp_buf[u] = mm(v_buf[yk], dt_buf[yq])
        total = r_buf[yq]
        for rows in chunks:
            total = total + fold(s_buf[u, rows, :] * dp_buf[u, rows, :], jnp.add)
        r_buf[yq] = total

    def prob_row(i, carry):
        yq = (y + i) % N_Y

        @pl.when(i > 0)
        def _():
            d_copy(i, yq).wait_recv()

        for h in range(GROUP_Q):
            rows = slice(h * BLOCK, (h + 1) * BLOCK)
            dt_buf[yq, :, rows] = d5_buf[yq, rows, :].astype(jnp.float32).T.astype(jnp.bfloat16)
        each_query(yq, lambda yk: prob_grads(yq, yk), lambda: prob_grads(yq, yq))
        return carry

    lax.fori_loop(0, N_Y, prob_row, 0)

    for i in range(1, N_Y):
        st_copy(i, (y + i) % N_Y).wait_recv()
    top_all = stat_buf[0, 0:N_Y, :]
    for t in range(1, N_Y):
        top_all = jnp.maximum(top_all, stat_buf[t, 0:N_Y, :])
    sum_all = jnp.zeros_like(top_all)
    for t in range(N_Y):
        sum_all = sum_all + stat_buf[t, N_Y : 2 * N_Y, :] * jnp.exp2(
            (stat_buf[t, 0:N_Y, :] - top_all) * factor
        )
    share = jnp.exp2((stat_buf[y, 0:N_Y, :] - top_all) * factor) / sum_all
    f_buf[0:N_Y, :] = share
    part_buf[y] = jnp.zeros((8, ROWS_Q), jnp.float32)
    for yq in range(N_Y):
        part_buf[y, yq : yq + 1, :] = (
            jnp.sum(r_buf[yq], axis=0, keepdims=True) * share[yq : yq + 1, :]
        )

    def pt_copy(i, owner):
        return remote(
            part_buf.at[owner], part_buf.at[owner], pt_send.at[i], pt_recv.at[owner], line(i)
        )

    for i in range(1, N_Y):
        pt_copy(i, y).start()

    def block_copy(which, yk, h):
        return remote(
            kv_send.at[which, 2 * yk + h],
            kv_recv.at[which, z],
            o_send.at[which, 2 * yk + h],
            o_recv.at[which, z],
            yk * N_Z + 2 * pair_of(yk) + h,
        )

    def give(which, yk, acc):
        for h in range(2):
            kv_send[which, 2 * yk + h] = acc[h * BLOCK : (h + 1) * BLOCK].astype(jnp.bfloat16)
            owner = yk * N_Z + 2 * pair_of(yk) + h

            @pl.when(owner != me)
            def _():
                block_copy(which, yk, h).start()

            @pl.when(owner == me)
            def _():
                kv_recv[which, z] = kv_send[which, 2 * yk + h]

    def value_grads(yq, yk):
        u = yq * N_Y + yk
        share_row = f_buf[pl.ds(yq, 1), :]
        for rows in chunks:
            prob = s_buf[u, rows, :] * share_row
            s_buf[u, rows, :] = prob
            p16_buf[rows, :] = prob.astype(jnp.bfloat16)
        dv_acc[yk] += mm(p16_buf[...], d5_buf[yq])

    def each_key(yk, full_step, own_step):
        def step(yq, carry):
            full_step(yq)
            return carry

        partly(yk, own_step)
        lax.fori_loop(yk + 1, N_Y, step, 0)

    def value_row(yk, carry):
        each_key(yk, lambda yq: value_grads(yq, yk), lambda: value_grads(yk, yk))
        give(0, yk, dv_acc[yk])
        return carry

    lax.fori_loop(0, N_Y, value_row, 0)

    for i in range(1, N_Y):
        pt_copy(i, (y + i) % N_Y).wait_recv()
    delta_buf[...] = part_buf[0] + part_buf[1] + part_buf[2] + part_buf[3]

    def key_grads(yq, yk):
        u = yq * N_Y + yk
        delta = delta_buf[pl.ds(yq, 1), :]
        for rows in chunks:
            ds16_buf[rows, :] = (
                s_buf[u, rows, :] * (dp_buf[u, rows, :] - delta)
            ).astype(jnp.bfloat16)
        ds16 = ds16_buf[...]
        dk_acc[yk] += mm(ds16, q5_ref[yq])
        dqt_buf[yq] += mm(kt_buf[yk], ds16)

    def dq_copy(yq):
        return remote(
            dq_send.at[yq], dq_recv.at[y], q_send.at[yq], q_recv.at[y], yq * N_Z + z
        )

    def key_row(yk, carry):
        each_key(yk, lambda yq: key_grads(yq, yk), lambda: key_grads(yk, yk))
        give(1, yk, dk_acc[yk] * scale)
        dq_send[yk] = (dqt_buf[yk] * scale).astype(jnp.bfloat16)

        @pl.when(yk != y)
        def _():
            dq_copy(yk).start()

        return carry

    lax.fori_loop(0, N_Y, key_row, 0)

    total = dq_send[y].astype(jnp.float32)
    for i in range(1, N_Y):
        peer = (y + i) % N_Y
        remote(
            dq_send.at[y], dq_recv.at[peer], q_send.at[y], q_recv.at[peer], line(i)
        ).wait_recv()
        total = total + dq_recv[peer].astype(jnp.float32)
    for h in range(GROUP_Q):
        cols = slice(h * BLOCK, (h + 1) * BLOCK)
        out_ref[:, cols] = total[:, cols].T.astype(jnp.bfloat16)

    for which, first in ((0, ROWS_Q + HD), (1, ROWS_Q)):
        total = jnp.zeros((BLOCK, HD), jnp.float32)
        for i in range(N_Z):
            peer = source_row * N_Z + i

            @pl.when(peer != me)
            def _():
                remote(
                    kv_send.at[which, 0], kv_recv.at[which, i], o_send.at[which, 0],
                    o_recv.at[which, i], peer,
                ).wait_recv()

            total = total + kv_recv[which, i].astype(jnp.float32)
        out_ref[:, first : first + HD] = total.astype(jnp.bfloat16)

    for i in range(1, N_Y):
        d_copy(i, y).wait_send()
        st_copy(i, y).wait_send()
        pt_copy(i, y).wait_send()
        dq_copy((y + i) % N_Y).wait_send()
    for which in range(2):
        for yk in range(N_Y):
            for h in range(2):

                @pl.when(yk * N_Z + 2 * pair_of(yk) + h != me)
                def _():
                    block_copy(which, yk, h).wait_send()


def attention(full_grad, q5, qt, kv, gathered):
    bf, f32 = jnp.bfloat16, jnp.float32
    vmem = pl.BlockSpec(memory_space=pltpu.VMEM)
    dma = pltpu.SemaphoreType.DMA
    units = N_Y * N_Y
    return pl.pallas_call(
        attention_kernel,
        name="attention_grads",
        out_shape=jax.ShapeDtypeStruct((BLOCK, ROWS_Q + 2 * HD), bf),
        in_specs=[vmem, vmem, vmem, vmem, pl.BlockSpec(memory_space=pl.ANY)],
        out_specs=vmem,
        scratch_shapes=[
            pltpu.VMEM((D, ROWS_Q), bf),
            pltpu.VMEM((N_Y, PAIR, HD), bf),
            pltpu.VMEM((N_Y, PAIR, HD), bf),
            pltpu.VMEM((N_Y, HD, PAIR), bf),
            pltpu.VMEM((N_Y, HD, ROWS_Q), bf),
            pltpu.VMEM((N_Y, ROWS_Q, HD), bf),
            pltpu.VMEM((units, PAIR, ROWS_Q), f32),
            pltpu.VMEM((units, PAIR, ROWS_Q), f32),
            pltpu.VMEM((PAIR, ROWS_Q), bf),
            pltpu.VMEM((PAIR, ROWS_Q), bf),
            pltpu.VMEM((N_Y, 8, ROWS_Q), f32),
            pltpu.VMEM((N_Y, 8, ROWS_Q), f32),
            pltpu.VMEM((N_Y, 8, ROWS_Q), f32),
            pltpu.VMEM((8, ROWS_Q), f32),
            pltpu.VMEM((8, ROWS_Q), f32),
            pltpu.VMEM((N_Y, 8, ROWS_Q), f32),
            pltpu.VMEM((N_Y, 8, ROWS_Q), f32),
            pltpu.VMEM((N_Y, HD, ROWS_Q), f32),
            pltpu.VMEM((N_Y, PAIR, HD), f32),
            pltpu.VMEM((N_Y, PAIR, HD), f32),
            pltpu.VMEM((N_Y, HD, ROWS_Q), bf),
            pltpu.VMEM((N_Y, HD, ROWS_Q), bf),
            pltpu.VMEM((2, 2 * N_Y, BLOCK, HD), bf),
            pltpu.VMEM((2, N_Z, BLOCK, HD), bf),
            dma,
            dma((N_Y,)), dma((N_Y,)),
            dma((N_Y,)), dma((N_Y,)),
            dma((N_Y,)), dma((N_Y,)),
            dma((N_Y,)), dma((N_Y,)),
            dma((2, 2 * N_Y)), dma((2, N_Z)),
        ],
        cost_estimate=pl.CostEstimate(
            flops=6_000_000_000, bytes_accessed=12_000_000, transcendentals=3_000_000
        ),
        compiler_params=pltpu.CompilerParams(
            collective_id=4, has_side_effects=True, vmem_limit_bytes=56 * 2**20
        ),
    )(full_grad, q5, qt, kv, gathered)


def dot_nt(a, b):
    return lax.dot_general(a, b, (((1,), (1,)), ((), ())), preferred_element_type=jnp.float32)


def expert_kernel(
    pack_ref, hidden_ref, grad_ref, q_ref, key_ref, value_ref,
    down_ref, gate_ref, up_ref, wg_ref, wu_ref,
    dh_ref, stat_ref, full_ref, q5_ref, qt_ref, kv_ref,
    down, wg, wu, slots_out, recv_d, flat, slots, own, sib_out, sib_in, x_out, x_in,
    prod_buf, gu, hid, acc, back, ret, rt_out, rt_in, terms, pick, picked, stats, square, full, q5, kv_out, kv,
    w_sem, d_send, d_recv, s_send, s_recv, x_send, x_recv, gx_send, gx_recv,
    gf_send, gf_recv, gs_send, gs_recv, ax_send, ax_recv, af_send, af_recv,
    as_send, as_recv, b_send, b_recv, t_send, t_recv, fx_send, fx_recv, fs_send, fs_recv,
    q_send, q_recv, k_send, k_recv, r_send, r_recv,
):
    me = lax.axis_index("ctx")
    tp = lax.axis_index("tp")
    y, z = me // N_Z, me % N_Z
    x, k = tp // 2, tp % 2
    sibling = 2 * x + (1 - k)
    far = (2, 1, 3)
    near = (1, 3)
    rows_by_chunk = (y, y + 1 - 2 * (y % 2), (y + 2) % N_Y, N_Y - 1 - y)

    def chip(dx):
        return (x + dx) % N_X

    def remote(src, dst, send, recv, ctx, peer):
        return pltpu.make_async_remote_copy(
            src_ref=src, dst_ref=dst, send_sem=send, recv_sem=recv,
            device_id=(ctx, peer), device_id_type=MESH,
        )

    barrier = pltpu.get_barrier_semaphore()

    def greet_ctx(i, carry):
        pl.semaphore_signal(
            barrier, inc=1, device_id=((me + i) % N_CTX, tp), device_id_type=MESH
        )
        return carry

    def greet_tp(i, carry):
        pl.semaphore_signal(
            barrier, inc=1, device_id=(me, (tp + i) % N_TP), device_id_type=MESH
        )
        return carry

    lax.fori_loop(1, N_CTX, greet_ctx, 0)
    lax.fori_loop(1, N_TP, greet_tp, 0)

    w_copies = [
        pltpu.make_async_copy(down_ref, down, w_sem.at[0]),
        pltpu.make_async_copy(wg_ref, wg, w_sem.at[1]),
        pltpu.make_async_copy(wu_ref, wu, w_sem.at[2]),
    ]
    for copy in w_copies:
        copy.start()

    def turn(row):
        return jnp.broadcast_to(row, (BLOCK, BLOCK)).T

    ids = jnp.broadcast_to(pack_ref[0:1, :], (BLOCK, BLOCK))
    ids_t = ids.T
    sub = lax.broadcasted_iota(jnp.int32, (BLOCK, BLOCK), 0)
    lan = lax.broadcasted_iota(jnp.int32, (BLOCK, BLOCK), 1)
    before = jnp.where((ids == ids_t) & (sub < lan), 1.0, 0.0)
    slot_row = pack_ref[0:1, :] * CAP + jnp.sum(before, axis=0, keepdims=True)
    slot_ids = lax.broadcasted_iota(jnp.int32, (EXPERTS * CAP, BLOCK), 0).astype(jnp.float32)
    placing = jnp.where(slot_ids == slot_row, 1.0, 0.0).astype(jnp.bfloat16)
    placed = mm(placing, grad_ref[...])
    for e in range(EXPERTS):
        slots_out[e] = placed[e * CAP : (e + 1) * CAP].astype(jnp.bfloat16)
    slot_col = turn(slot_row)[:, 0:1]
    number = lax.broadcasted_iota(jnp.int32, (8, N_Y * N_Z * CAP_PAD), 1).astype(jnp.float32)
    device_row = jnp.floor((number + 0.5) / (N_Z * CAP_PAD))
    within = number - device_row * (N_Z * CAP_PAD)
    device = jnp.floor((within + 0.5) / CAP)
    column = (
        jnp.floor((device_row * N_Z + device + 0.5) / GROUP) * CAP + within - device * CAP
    )
    column = jnp.where(within < CHUNK, column, -1.0)
    pick[...] = jnp.where(column[0:1, :] == slot_col, 1.0, 0.0).astype(jnp.bfloat16)
    score = turn(pack_ref[1:2, :])[:, 0:1]
    gain_val = jnp.concatenate([pack_ref[2 + h : 3 + h, :] for h in range(GROUP_Q)], axis=1)

    gate = gate_ref[...].astype(jnp.float32).T
    up = up_ref[...].astype(jnp.float32).T
    act, slope = silu_parts(gate)
    gu[tp, :, 0:FF_DEV] = (up * slope).astype(jnp.bfloat16)
    gu[tp, :, FF_DEV : 2 * FF_DEV] = act.astype(jnp.bfloat16)
    prod_buf[...] = act * up
    spot = lax.broadcasted_iota(jnp.int32, (CHUNK, BLOCK), 0).astype(jnp.float32)
    spot = spot - CAP * jnp.floor((spot + 0.5) / CAP)
    spot_is = jnp.where(
        spot == lax.broadcasted_iota(jnp.int32, (CHUNK, BLOCK), 1).astype(jnp.float32), 1.0, 0.0
    )
    own_sub = lax.broadcasted_iota(jnp.int32, (N_Z, CHUNK), 0) * CAP
    own_lan = lax.broadcasted_iota(jnp.int32, (N_Z, CHUNK), 1)
    owner_is = jnp.where((own_lan >= own_sub) & (own_lan < own_sub + CAP), 1.0, 0.0)
    owner_is = owner_is.astype(jnp.bfloat16)
    for h in range(GROUP_Q):
        heads = slice(h * BLOCK, (h + 1) * BLOCK)
        q5[y, heads, :] = q_ref[:, heads]
    kv_out[0] = key_ref[...]
    kv_out[1] = value_ref[...]
    hidden_val = hidden_ref[...].astype(jnp.float32)
    square[...] = jnp.broadcast_to(
        jnp.sum(hidden_val * hidden_val, axis=1, keepdims=True), square.shape
    )
    pl.semaphore_wait(barrier, N_CTX - 1 + N_TP - 1)

    def exchange(buf, x_s, x_r, f_s, f_r, s_s, s_r):
        def send_near(ch):
            rows = chunk_rows(ch)
            for i, dx in enumerate(near):
                remote(
                    buf.at[tp, rows], buf.at[tp, rows], x_s.at[i, ch], x_r.at[i, ch],
                    me, 2 * chip(dx) + k,
                ).start()
            share(tp, 3, ch).start()

        def source(i):
            return 2 * chip(N_X - near[i]) + k

        def share(t, i, ch):
            rows = chunk_rows(ch)
            return remote(
                buf.at[t, rows], buf.at[t, rows], s_s.at[i, ch], s_r.at[i, ch], me, sibling
            )

        def half(i, ch):
            start = rows_by_chunk[ch] * CHUNK + i * (CHUNK // 2)
            return pl.ds(pl.multiple_of(start, CHUNK // 2), CHUNK // 2)

        def pass_on(i, ch):
            rows = half(i, ch)
            t = source(i)
            return remote(
                buf.at[t, rows], buf.at[t, rows], f_s.at[i, ch], f_r.at[i, ch],
                me, 2 * chip(near[i]) + k,
            )

        def get_near(ch):
            rows = chunk_rows(ch)
            for i in range(2):
                t = source(i)
                remote(
                    buf.at[t, rows], buf.at[t, rows], x_s.at[i, ch], x_r.at[i, ch], me, t
                ).wait_recv()
                pass_on(i, ch).start()
                share(t, i, ch).start()

        opposite = 2 * chip(2) + k

        def get_far(ch):
            for i in range(2):
                rows = half(i, ch)
                remote(
                    buf.at[opposite, rows], buf.at[opposite, rows], f_s.at[i, ch], f_r.at[i, ch],
                    me, opposite,
                ).wait_recv()
            share(opposite, 2, ch).start()

        def shared(i):
            return (source(0), source(1), opposite, tp)[i] + 1 - 2 * k

        def get_shared(i, ch):
            share(shared(i), i, ch).wait_recv()

        def drain(ch):
            rows = chunk_rows(ch)
            for i in range(2):
                remote(
                    buf.at[tp, rows], buf.at[tp, rows], x_s.at[i, ch], x_r.at[i, ch],
                    me, 2 * chip(near[i]) + k,
                ).wait_send()
                pass_on(i, ch).wait_send()
            for i in range(4):
                share(tp, i, ch).wait_send()

        return send_near, get_near, get_far, get_shared, drain, source, opposite, shared

    def chunk_rows(ch):
        return pl.ds(pl.multiple_of(rows_by_chunk[ch] * CHUNK, CHUNK), CHUNK)

    def pair_first(p):
        return 2 * (y // 2) if p == 0 else 2 - 2 * (y // 2)

    def pair_rows(p):
        return pl.ds(pl.multiple_of(pair_first(p) * CHUNK, PAIR_ROWS), PAIR_ROWS)

    gu_x = exchange(gu, gx_send, gx_recv, gf_send, gf_recv, gs_send, gs_recv)
    hid_x = exchange(hid, ax_send, ax_recv, af_send, af_recv, as_send, as_recv)
    source, opposite, shared = hid_x[5:]

    def dispatch(j):
        return remote(
            slots_out.at[j // GROUP], recv_d.at[me], d_send.at[j], d_recv.at[me], j, tp
        )

    def dispatch_row(ch):
        row = rows_by_chunk[ch]

        def send_step(dz, carry):
            dispatch(row * N_Z + (z + dz) % N_Z).start()
            return carry

        lax.fori_loop(1 if ch == 0 else 0, N_Z, send_step, 0)

    recv_d[me] = slots_out[me // GROUP]

    def q_copy(i, owner):
        ctx = ((y + i) % N_Y) * N_Z + z
        return remote(q5.at[owner], q5.at[owner], q_send.at[i], q_recv.at[owner], ctx, tp)

    def turn_queries():
        for i in range(1, N_Y):
            q_copy(i, (y + i) % N_Y).wait_recv()
        q5_ref[...] = q5[...]
        for r in range(N_Y):
            for h in range(GROUP_Q):
                heads = slice(h * BLOCK, (h + 1) * BLOCK)
                qt_ref[r, :, heads] = q5[r, heads, :].astype(jnp.float32).T.astype(jnp.bfloat16)

    user_row = (y - z // 2 + N_Y) % N_Y

    def kv_copy(i):
        return remote(
            kv_out, kv.at[y, z % 2], k_send.at[i], k_recv.at[y, z % 2], user_row * N_Z + i, tp
        )

    def send_keys():
        for i in range(N_Z):

            @pl.when(user_row * N_Z + i != me)
            def _():
                kv_copy(i).start()

        @pl.when(user_row == y)
        def _():
            kv[y, z % 2] = kv_out[...]

    def get_keys():
        for r in range(N_Y):
            for h in range(2):
                peer = r * N_Z + 2 * ((r - y + N_Y) % N_Y) + h

                @pl.when(peer != me)
                def _():
                    remote(
                        kv_out, kv.at[r, h], k_send.at[0], k_recv.at[r, h], peer, tp
                    ).wait_recv()

        kv_ref[...] = kv[...]

    def arrive(ch):
        first = rows_by_chunk[ch] * N_Z
        for i in range(N_Z):
            j = first + i

            @pl.when(j != me)
            def _():
                remote(
                    slots_out.at[0], recv_d.at[j], d_send.at[j], d_recv.at[j], j, tp
                ).wait_recv()

            flat[i * CAP : (i + 1) * CAP, :] = recv_d[j].astype(jnp.float32)
        slots[chunk_rows(ch), :] = flat[...].astype(jnp.bfloat16)

    def sib_copy(i, ch):
        rows = chunk_rows(ch)
        return remote(
            sib_out.at[i, rows], sib_in.at[i, rows], s_send.at[i, ch], s_recv.at[i, ch],
            me, sibling,
        )

    def x_copy(i, ch):
        rows = chunk_rows(ch)
        return remote(
            x_out.at[i, rows], x_in.at[i, rows], x_send.at[i, ch], x_recv.at[i, ch],
            me, 2 * chip(far[i]) + k,
        )

    def stage1(ch):
        rows = chunk_rows(ch)
        part = slots[rows, :]
        for i, dx in enumerate(far + (0,)):
            base = 2 * chip(dx)

            def block(t):
                start = pl.multiple_of(t * FF_DEV, FF_DEV)
                return dot_nt(part, down[pl.ds(start, FF_DEV), :]).astype(jnp.bfloat16)

            sib_out[i, rows, :] = block(base + 1 - k)
            sib_copy(i, ch).start()
            own[i, rows, :] = block(base + k)

    def joined(i, ch):
        rows = chunk_rows(ch)
        sib_copy(i, ch).wait_recv()
        return own[i, rows, :].astype(jnp.float32) + sib_in[i, rows, :].astype(jnp.float32)

    def stage2(ch):
        rows = chunk_rows(ch)
        for i in range(3):
            x_out[i, rows, :] = joined(i, ch).astype(jnp.bfloat16)
            x_copy(i, ch).start()

    def rt_copy(j, ch):
        return remote(rt_out.at[ch], rt_in.at[me], r_send.at[j], r_recv.at[me], j, tp)

    def stage3(ch):
        rows = chunk_rows(ch)
        total = joined(3, ch)
        for i in range(3):
            x_copy(i, ch).wait_recv()
            total = total + x_in[i, rows, :].astype(jnp.float32)
        hid[tp, rows, :] = total.astype(jnp.bfloat16)
        hid_x[0](ch)
        term = jnp.sum(total * prod_buf[rows, :], axis=1, keepdims=True)
        rt_out[ch] = mm(owner_is, (term * spot_is).astype(jnp.bfloat16))
        for i in range(N_Z):
            j = rows_by_chunk[ch] * N_Z + i

            @pl.when(j != me)
            def _():
                rt_copy(j, ch).start()

        if ch == 0:
            rt_in[me] = rt_out[0]

    def product(t, p):
        rows = pair_rows(p)
        cols = pl.ds(pl.multiple_of(t * FF_DEV, FF_DEV), FF_DEV)
        val = hid[t, rows, :].astype(jnp.float32)
        grad_gate = (val * gu[t, rows, 0:FF_DEV].astype(jnp.float32)).astype(jnp.bfloat16)
        grad_up = (val * gu[t, rows, FF_DEV : 2 * FF_DEV].astype(jnp.float32)).astype(jnp.bfloat16)
        return dot_nt(grad_gate, wg[:, cols]) + dot_nt(grad_up, wu[:, cols])

    def back_copy(j):
        return remote(back.at[j], ret.at[me], b_send.at[j], b_recv.at[me], j, tp)

    def near_products(p):
        acc[p] = product(tp, p)
        for i in range(2):
            acc[p] += product(source(i), p)

    def far_products(p):
        acc[p] += product(opposite, p)
        for i in (3, 0, 1, 2):
            for ch in (2 * p, 2 * p + 1):
                hid_x[3](i, ch)
            acc[p] += product(shared(i), p)

    def give_back(p):
        for i in range(2 * N_Z):
            j = pair_first(p) * N_Z + i
            back[j] = acc[p, i * CAP : (i + 1) * CAP, :].astype(jnp.bfloat16)

            @pl.when(j != me)
            def _():
                back_copy(j).start()

    for ch in range(2):
        dispatch_row(ch)
    for ch in range(N_Y):
        gu_x[0](ch)
    for ch in range(2, N_Y):
        dispatch_row(ch)
    w_copies[0].wait()
    arrive(0)
    stage1(0)
    gu_x[1](0)
    arrive(1)
    stage1(1)
    stage2(0)
    gu_x[1](1)
    arrive(2)
    stage1(2)
    stage2(1)
    gu_x[1](2)
    arrive(3)
    for i in range(1, N_Y):
        q_copy(i, y).start()
    send_keys()
    stage1(3)
    stage2(2)
    gu_x[1](3)
    stage2(3)
    for ch in range(N_Y):
        gu_x[2](ch)
    for ch in range(N_Y):
        stage3(ch)
    for ch in range(N_Y):
        for i in range(4):
            gu_x[3](i, ch)
    w_copies[1].wait()
    w_copies[2].wait()
    hid_x[1](0)
    hid_x[1](1)
    near_products(0)
    hid_x[2](0)
    hid_x[2](1)
    hid_x[1](2)
    hid_x[1](3)
    far_products(0)
    give_back(0)
    near_products(1)
    hid_x[2](2)
    hid_x[2](3)
    far_products(1)
    give_back(1)
    ret[me] = back[me]
    turn_queries()
    get_keys()

    for j in range(N_CTX):

        @pl.when(j != me)
        def _():
            remote(rt_out.at[0], rt_in.at[j], r_send.at[j], r_recv.at[j], j, tp).wait_recv()

        terms[j : j + 1, :] = rt_in[j, pl.ds(z, 1), :]
    expert_col = turn(pack_ref[0:1, :])[:, 0:1]
    rank_col = slot_col - CAP * expert_col
    member = lax.broadcasted_iota(jnp.int32, (BLOCK, N_CTX), 1)
    member = jnp.floor((member.astype(jnp.float32) + 0.5) / GROUP)
    member_is = jnp.where(member == expert_col, 1.0, 0.0).astype(jnp.bfloat16)
    token_terms = mm(member_is, terms[...].astype(jnp.bfloat16))
    router_tok = jnp.sum(
        jnp.where(lan.astype(jnp.float32) == rank_col, token_terms, 0.0), axis=1, keepdims=True
    )
    picked[...] = jnp.zeros_like(picked)
    for ch in range(N_Y):
        first = rows_by_chunk[ch] * N_Z
        for i in range(N_Z):
            j = first + i

            @pl.when(j != me)
            def _():
                remote(back.at[j], ret.at[j], b_send.at[j], b_recv.at[j], j, tp).wait_recv()

            flat[i * CAP : (i + 1) * CAP, :] = ret[j].astype(jnp.float32)
        cols = pl.ds(pl.multiple_of(first * CAP_PAD, N_Z * CAP_PAD), N_Z * CAP_PAD)
        picked[...] += mm(pick[:, cols][:, 0:CHUNK], flat[...].astype(jnp.bfloat16))

    norm_grad = picked[...] * score
    hidden_now = hidden_ref[...].astype(jnp.float32)
    cross = jnp.sum(hidden_now * gain_val * norm_grad, axis=1, keepdims=True)
    packed = jnp.where(
        lan == 0, router_tok, jnp.where(lan == 1, square[...], cross)
    )
    stats[tp] = packed.T[0:8, :]

    def stat_copy(peer, src):
        return remote(
            stats.at[src], stats.at[src], t_send.at[peer], t_recv.at[src], me, peer
        )

    def stat_start(i, carry):
        stat_copy((tp + i) % N_TP, tp).start()
        return carry

    def stat_wait(i, carry):
        stat_copy((tp + i) % N_TP, (tp + i) % N_TP).wait_recv()
        return carry

    lax.fori_loop(1, N_TP, stat_start, 0)
    lax.fori_loop(1, N_TP, stat_wait, 0)
    total = stats[0]
    for t in range(1, N_TP):
        total = total + stats[t]
    stat_ref[...] = total
    spread = jnp.concatenate([total] * (BLOCK // 8), axis=0).T
    inverse_rms = lax.rsqrt(spread[:, 1:2] / D + EPSILON)
    cross_sum = spread[:, 2:3]
    d_hidden = (
        grad_ref[...].astype(jnp.float32)
        + inverse_rms * gain_val * norm_grad
        - hidden_now * inverse_rms * inverse_rms * inverse_rms * cross_sum / D
    ).astype(jnp.bfloat16)
    dh_ref[...] = d_hidden
    full[tp] = d_hidden

    def full_chip(i):
        return 2 * chip(N_X - far[i]) + k

    def full_out(i):
        return remote(
            full.at[tp], full.at[tp], fx_send.at[i], fx_recv.at[i], me, 2 * chip(far[i]) + k
        )

    def full_share(t, i):
        return remote(full.at[t], full.at[t], fs_send.at[i], fs_recv.at[i], me, sibling)

    for i in range(3):
        full_out(i).start()
    full_share(tp, 3).start()
    for i in (1, 2, 0):
        t = full_chip(i)
        remote(full.at[t], full.at[t], fx_send.at[i], fx_recv.at[i], me, t).wait_recv()
        full_share(t, i).start()
    for i in (3, 1, 2, 0):
        t = sibling if i == 3 else full_chip(i) + 1 - 2 * k
        full_share(t, i).wait_recv()
    full_ref[...] = full[...]

    def drain_ctx(i, carry):
        j = (me + i) % N_CTX
        dispatch(j).wait_send()
        back_copy(j).wait_send()
        rt_copy(j, 0).wait_send()
        return carry

    def drain_tp(i, carry):
        stat_copy((tp + i) % N_TP, tp).wait_send()
        return carry

    lax.fori_loop(1, N_CTX, drain_ctx, 0)
    lax.fori_loop(1, N_TP, drain_tp, 0)
    for ch in range(N_Y):
        for i in range(4):
            sib_copy(i, ch).wait_send()
        for i in range(3):
            x_copy(i, ch).wait_send()
        gu_x[4](ch)
        hid_x[4](ch)
    for i in range(1, N_Y):
        q_copy(i, y).wait_send()
    for i in range(N_Z):

        @pl.when(user_row * N_Z + i != me)
        def _():
            kv_copy(i).wait_send()

    for i in range(3):
        full_out(i).wait_send()
    for i in range(4):
        full_share(tp, i).wait_send()


def expert_block(pack, hidden, grad, queries, keys, values, down, gate, up, wg, wu):
    bf, f32 = jnp.bfloat16, jnp.float32
    vmem = pl.BlockSpec(memory_space=pltpu.VMEM)
    hbm = pl.BlockSpec(memory_space=pl.ANY)
    dma = pltpu.SemaphoreType.DMA
    return pl.pallas_call(
        expert_kernel,
        name="expert_block",
        out_shape=[
            jax.ShapeDtypeStruct((BLOCK, FEAT), bf),
            jax.ShapeDtypeStruct((8, BLOCK), f32),
            jax.ShapeDtypeStruct((N_TP, BLOCK, FEAT), bf),
            jax.ShapeDtypeStruct((N_Y, ROWS_Q, HD), bf),
            jax.ShapeDtypeStruct((N_Y, HD, ROWS_Q), bf),
            jax.ShapeDtypeStruct((N_Y, 2, 2, BLOCK, HD), bf),
        ],
        in_specs=[vmem] * 6 + [hbm, vmem, vmem, hbm, hbm],
        out_specs=[vmem] * 6,
        scratch_shapes=[
            pltpu.VMEM((FF_GRP, FEAT), bf),
            pltpu.VMEM((FEAT, FF_GRP), bf),
            pltpu.VMEM((FEAT, FF_GRP), bf),
            pltpu.VMEM((EXPERTS, CAP, FEAT), bf),
            pltpu.VMEM((N_CTX, CAP, FEAT), bf),
            pltpu.VMEM((CHUNK, FEAT), f32),
            pltpu.VMEM((SLOTS, FEAT), bf),
            pltpu.VMEM((4, SLOTS, FF_DEV), bf),
            pltpu.VMEM((4, SLOTS, FF_DEV), bf),
            pltpu.VMEM((4, SLOTS, FF_DEV), bf),
            pltpu.VMEM((3, SLOTS, FF_DEV), bf),
            pltpu.VMEM((3, SLOTS, FF_DEV), bf),
            pltpu.VMEM((SLOTS, FF_DEV), f32),
            pltpu.VMEM((N_TP, SLOTS, 2 * FF_DEV), bf),
            pltpu.VMEM((N_TP, SLOTS, FF_DEV), bf),
            pltpu.VMEM((2, PAIR_ROWS, FEAT), f32),
            pltpu.VMEM((N_CTX, CAP, FEAT), bf),
            pltpu.VMEM((N_CTX, CAP, FEAT), bf),
            pltpu.VMEM((N_Y, N_Z, BLOCK), f32),
            pltpu.VMEM((N_CTX, N_Z, BLOCK), f32),
            pltpu.VMEM((N_CTX, BLOCK), f32),
            pltpu.VMEM((BLOCK, N_Y * N_Z * CAP_PAD), bf),
            pltpu.VMEM((BLOCK, FEAT), f32),
            pltpu.VMEM((N_TP, 8, BLOCK), f32),
            pltpu.VMEM((BLOCK, HD), f32),
            pltpu.VMEM((N_TP, BLOCK, FEAT), bf),
            pltpu.VMEM((N_Y, ROWS_Q, HD), bf),
            pltpu.VMEM((2, BLOCK, HD), bf),
            pltpu.VMEM((N_Y, 2, 2, BLOCK, HD), bf),
            dma((3,)),
            dma((N_CTX,)), dma((N_CTX,)),
            dma((4, N_Y)), dma((4, N_Y)),
            dma((3, N_Y)), dma((3, N_Y)),
            dma((2, N_Y)), dma((2, N_Y)),
            dma((2, N_Y)), dma((2, N_Y)),
            dma((4, N_Y)), dma((4, N_Y)),
            dma((2, N_Y)), dma((2, N_Y)),
            dma((2, N_Y)), dma((2, N_Y)),
            dma((4, N_Y)), dma((4, N_Y)),
            dma((N_CTX,)), dma((N_CTX,)),
            dma((N_TP,)), dma((N_TP,)),
            dma((3,)), dma((3,)),
            dma((4,)), dma((4,)),
            dma((N_Y,)), dma((N_Y,)),
            dma((N_Z,)), dma((N_Y, 2)),
            dma((N_CTX,)), dma((N_CTX,)),
        ],
        cost_estimate=pl.CostEstimate(
            flops=60_000_000_000, bytes_accessed=200_000_000, transcendentals=3_000_000
        ),
        compiler_params=pltpu.CompilerParams(
            collective_id=3, has_side_effects=True, vmem_limit_bytes=56 * 2**20
        ),
    )(pack, hidden, grad, queries, keys, values, down, gate, up, wg, wu)


def body(
    hidden_in,
    norm_gain,
    out_grad,
    router_score,
    expert_ids,
    gate_saved,
    up_saved,
    w_gate,
    w_up,
    w_down,
    w_out,
    queries,
    keys,
    values,
):
    gathered = lax.all_gather(w_out.T, "ctx", axis=0, tiled=True)
    pack = jnp.concatenate(
        [
            expert_ids.reshape(1, BLOCK).astype(jnp.float32),
            router_score.astype(jnp.float32).reshape(1, BLOCK),
            norm_gain.astype(jnp.float32).reshape(GROUP_Q, BLOCK),
            jnp.zeros((1, BLOCK), jnp.float32),
        ],
        axis=0,
    )
    d_hidden, stats, full_grad, q5, qt, kv = expert_block(
        pack,
        hidden_in,
        out_grad,
        queries,
        keys,
        values,
        w_down[0],
        gate_saved[0],
        up_saved[0],
        w_gate[0],
        w_up[0],
    )
    router_grad = stats[0]
    grads = attention(full_grad, q5, qt, kv, gathered)
    query_grad = grads[:, 0:ROWS_Q]
    key_grad = grads[:, ROWS_Q : ROWS_Q + HD]
    value_grad = grads[:, ROWS_Q + HD :]
    return (
        d_hidden,
        router_grad,
        query_grad,
        key_grad,
        value_grad,
    )


def solution(mesh):
    in_specs = (
        P("ctx", "tp"),
        P("tp"),
        P("ctx", "tp"),
        P("ctx"),
        P("ctx", None),
        P("ctx", "tp", None),
        P("ctx", "tp", None),
        P("ctx", "tp", None),
        P("ctx", "tp", None),
        P("ctx", None, "tp"),
        P("tp", "ctx"),
        P("ctx", "tp"),
        P("ctx", "tp"),
        P("ctx", "tp"),
    )
    out_specs = (P("ctx", "tp"), P("ctx"), P("ctx", "tp"), P("ctx", "tp"), P("ctx", "tp"))
    return jax.shard_map(body, mesh=mesh, in_specs=in_specs, out_specs=out_specs, check_vma=False)
```

```python
import jax
import jax.numpy as jnp
from jax import lax
from jax.experimental import pallas as pl
from jax.experimental.pallas import tpu as pltpu
from jax.sharding import PartitionSpec as P

D = 5120
QH = 40
KVH = 8
HD = 128
EXPERTS = 8
GROUP_Q = QH // KVH
N_CTX = 32
BLOCK = 128
PAIR = 2 * BLOCK
ROWS_Q = GROUP_Q * BLOCK
N_Y, N_Z, N_X, N_TP = 4, 8, 4, 8
W_ROWS = D // N_CTX
GROUP = N_CTX // EXPERTS
CAP = 24
CAP_PAD = 32
CHUNK = N_Z * CAP
SLOTS = N_CTX * CAP
FEAT = D // N_TP
FF_GRP = 2048
FF_DEV = FF_GRP // N_TP
PAIR_ROWS = 2 * CHUNK
MESH = pl.DeviceIdType.MESH
EPSILON = 1e-05
NEG = -1e30
LOG2E = 1.4426950408889634


def silu_parts(gate_pre):
    sigmoid_val = jax.nn.sigmoid(gate_pre)
    return (gate_pre * sigmoid_val, sigmoid_val * (1.0 + gate_pre * (1.0 - sigmoid_val)))


def mm(a, b):
    return jnp.dot(a, b, preferred_element_type=jnp.float32)


def attention_kernel(
    full_ref, q5_ref, qt_ref, kv_ref, gathered_ref, out_ref,
    w_buf, k_buf, v_buf, kt_buf, dt_buf, d5_buf, s_buf, dp_buf, p16_buf, ds16_buf,
    m_buf, l_buf, r_buf, f_buf, delta_buf, stat_buf, part_buf, dqt_buf, dk_acc, dv_acc,
    dq_send, dq_recv, kv_send, kv_recv,
    w_sem, d_send, d_recv, st_send, st_recv, pt_send, pt_recv,
    q_send, q_recv, o_send, o_recv,
):
    me = lax.axis_index("ctx")
    tp = lax.axis_index("tp")
    y, z = me // N_Z, me % N_Z
    scale = HD ** -0.5
    factor = scale * LOG2E

    def line(i):
        return ((y + i) % N_Y) * N_Z + z

    def pair_of(yk):
        return (yk - y + N_Y) % N_Y

    def remote(src, dst, send, recv, ctx):
        return pltpu.make_async_remote_copy(
            src_ref=src, dst_ref=dst, send_sem=send, recv_sem=recv,
            device_id=(ctx, tp), device_id_type=MESH,
        )

    source_row = (y - z // 2 + N_Y) % N_Y
    barrier = pltpu.get_barrier_semaphore()
    for i in range(1, N_Y):
        pl.semaphore_signal(barrier, inc=1, device_id=(line(i), tp), device_id_type=MESH)
    for i in range(N_Z):
        peer = source_row * N_Z + i

        @pl.when(peer != me)
        def _():
            pl.semaphore_signal(barrier, inc=1, device_id=(peer, tp), device_id_type=MESH)

    w_copy = pltpu.make_async_copy(gathered_ref, w_buf, w_sem)
    w_copy.start()
    for yk in range(N_Y):
        for h in range(2):
            rows = slice(h * BLOCK, (h + 1) * BLOCK)
            k_buf[yk, rows, :] = kv_ref[yk, h, 0]
            v_buf[yk, rows, :] = kv_ref[yk, h, 1]
        kt_buf[yk] = k_buf[yk].astype(jnp.float32).T.astype(jnp.bfloat16)
    m_buf[...] = jnp.full(m_buf.shape, NEG, jnp.float32)
    for ref in (l_buf, r_buf, dqt_buf, dk_acc, dv_acc):
        ref[...] = jnp.zeros_like(ref)

    w_copy.wait()
    dout = mm(full_ref[0], w_buf[0:FEAT, :])
    for t in range(1, N_TP):
        dout = dout + mm(full_ref[t], w_buf[t * FEAT : (t + 1) * FEAT, :])
    dout = dout.astype(jnp.bfloat16)
    for h in range(GROUP_Q):
        rows = slice(h * BLOCK, (h + 1) * BLOCK)
        d5_buf[y, rows, :] = dout[:, rows]

    pl.semaphore_wait(barrier, N_Y - 1 + N_Z - jnp.where(z < 2, 1, 0))

    def d_copy(i, owner):
        return remote(d5_buf.at[owner], d5_buf.at[owner], d_send.at[i], d_recv.at[owner], line(i))

    for i in range(1, N_Y):
        d_copy(i, y).start()

    def fold(x, op):
        total = x[0:8]
        for i in range(1, x.shape[0] // 8):
            total = op(total, x[8 * i : 8 * i + 8])
        return total

    def partly(yk, step):
        @pl.when(2 * pair_of(yk) <= z)
        def _():
            step()

    step_rows = 32
    chunks = [slice(i * step_rows, (i + 1) * step_rows) for i in range(PAIR // step_rows)]

    def scores(yq, yk, masked):
        u = yq * N_Y + yk
        s_buf[u] = mm(k_buf[yk], qt_ref[yq])
        top = m_buf[yq]
        for rows in chunks:
            part = s_buf[u, rows, :]
            if masked:
                shape = (step_rows, ROWS_Q)
                key_pos = lax.broadcasted_iota(jnp.int32, shape, 0) + rows.start
                row_pos = lax.broadcasted_iota(jnp.int32, shape, 1) % BLOCK
                part = jnp.where(key_pos <= row_pos + (z - 2 * pair_of(yk)) * BLOCK, part, NEG)
                s_buf[u, rows, :] = part
            top = jnp.maximum(top, fold(part, jnp.maximum))
        m_buf[yq] = top

    def exponents(yq, yk):
        u = yq * N_Y + yk
        top = stat_buf[y, pl.ds(yq, 1), :]
        total = l_buf[yq]
        for rows in chunks:
            e = jnp.exp2((s_buf[u, rows, :] - top) * factor)
            s_buf[u, rows, :] = e
            total = total + fold(e, jnp.add)
        l_buf[yq] = total

    def each_query(yq, full_step, own_step):
        def step(yk, carry):
            full_step(yk)
            return carry

        lax.fori_loop(0, yq, step, 0)
        partly(yq, own_step)

    def score_row(yq, carry):
        each_query(yq, lambda yk: scores(yq, yk, False), lambda: scores(yq, yq, True))
        return carry

    lax.fori_loop(0, N_Y, score_row, 0)
    for yq in range(N_Y):
        stat_buf[y, yq : yq + 1, :] = jnp.max(m_buf[yq], axis=0, keepdims=True)

    def exponent_row(yq, carry):
        each_query(yq, lambda yk: exponents(yq, yk), lambda: exponents(yq, yq))
        return carry

    lax.fori_loop(0, N_Y, exponent_row, 0)
    for yq in range(N_Y):
        stat_buf[y, N_Y + yq : N_Y + yq + 1, :] = jnp.sum(l_buf[yq], axis=0, keepdims=True)

    def st_copy(i, owner):
        return remote(
            stat_buf.at[owner], stat_buf.at[owner], st_send.at[i], st_recv.at[owner], line(i)
        )

    for i in range(1, N_Y):
        st_copy(i, y).start()

    def prob_grads(yq, yk):
        u = yq * N_Y + yk
        dp_buf[u] = mm(v_buf[yk], dt_buf[yq])
        total = r_buf[yq]
        for rows in chunks:
            total = total + fold(s_buf[u, rows, :] * dp_buf[u, rows, :], jnp.add)
        r_buf[yq] = total

    def prob_row(i, carry):
        yq = (y + i) % N_Y

        @pl.when(i > 0)
        def _():
            d_copy(i, yq).wait_recv()

        for h in range(GROUP_Q):
            rows = slice(h * BLOCK, (h + 1) * BLOCK)
            dt_buf[yq, :, rows] = d5_buf[yq, rows, :].astype(jnp.float32).T.astype(jnp.bfloat16)
        each_query(yq, lambda yk: prob_grads(yq, yk), lambda: prob_grads(yq, yq))
        return carry

    lax.fori_loop(0, N_Y, prob_row, 0)

    for i in range(1, N_Y):
        st_copy(i, (y + i) % N_Y).wait_recv()
    top_all = stat_buf[0, 0:N_Y, :]
    for t in range(1, N_Y):
        top_all = jnp.maximum(top_all, stat_buf[t, 0:N_Y, :])
    sum_all = jnp.zeros_like(top_all)
    for t in range(N_Y):
        sum_all = sum_all + stat_buf[t, N_Y : 2 * N_Y, :] * jnp.exp2(
            (stat_buf[t, 0:N_Y, :] - top_all) * factor
        )
    share = jnp.exp2((stat_buf[y, 0:N_Y, :] - top_all) * factor) / sum_all
    f_buf[0:N_Y, :] = share
    part_buf[y] = jnp.zeros((8, ROWS_Q), jnp.float32)
    for yq in range(N_Y):
        part_buf[y, yq : yq + 1, :] = (
            jnp.sum(r_buf[yq], axis=0, keepdims=True) * share[yq : yq + 1, :]
        )

    def pt_copy(i, owner):
        return remote(
            part_buf.at[owner], part_buf.at[owner], pt_send.at[i], pt_recv.at[owner], line(i)
        )

    for i in range(1, N_Y):
        pt_copy(i, y).start()

    def block_copy(which, yk, h):
        return remote(
            kv_send.at[which, 2 * yk + h],
            kv_recv.at[which, z],
            o_send.at[which, 2 * yk + h],
            o_recv.at[which, z],
            yk * N_Z + 2 * pair_of(yk) + h,
        )

    def give(which, yk, acc):
        for h in range(2):
            kv_send[which, 2 * yk + h] = acc[h * BLOCK : (h + 1) * BLOCK].astype(jnp.bfloat16)
            owner = yk * N_Z + 2 * pair_of(yk) + h

            @pl.when(owner != me)
            def _():
                block_copy(which, yk, h).start()

            @pl.when(owner == me)
            def _():
                kv_recv[which, z] = kv_send[which, 2 * yk + h]

    def value_grads(yq, yk):
        u = yq * N_Y + yk
        share_row = f_buf[pl.ds(yq, 1), :]
        for rows in chunks:
            prob = s_buf[u, rows, :] * share_row
            s_buf[u, rows, :] = prob
            p16_buf[rows, :] = prob.astype(jnp.bfloat16)
        dv_acc[yk] += mm(p16_buf[...], d5_buf[yq])

    def each_key(yk, full_step, own_step):
        def step(yq, carry):
            full_step(yq)
            return carry

        partly(yk, own_step)
        lax.fori_loop(yk + 1, N_Y, step, 0)

    def value_row(yk, carry):
        each_key(yk, lambda yq: value_grads(yq, yk), lambda: value_grads(yk, yk))
        give(0, yk, dv_acc[yk])
        return carry

    lax.fori_loop(0, N_Y, value_row, 0)

    for i in range(1, N_Y):
        pt_copy(i, (y + i) % N_Y).wait_recv()
    delta_buf[...] = part_buf[0] + part_buf[1] + part_buf[2] + part_buf[3]

    def key_grads(yq, yk):
        u = yq * N_Y + yk
        delta = delta_buf[pl.ds(yq, 1), :]
        for rows in chunks:
            ds16_buf[rows, :] = (
                s_buf[u, rows, :] * (dp_buf[u, rows, :] - delta)
            ).astype(jnp.bfloat16)
        ds16 = ds16_buf[...]
        dk_acc[yk] += mm(ds16, q5_ref[yq])
        dqt_buf[yq] += mm(kt_buf[yk], ds16)

    def dq_copy(yq):
        return remote(
            dq_send.at[yq], dq_recv.at[y], q_send.at[yq], q_recv.at[y], yq * N_Z + z
        )

    def key_row(yk, carry):
        each_key(yk, lambda yq: key_grads(yq, yk), lambda: key_grads(yk, yk))
        give(1, yk, dk_acc[yk] * scale)
        dq_send[yk] = (dqt_buf[yk] * scale).astype(jnp.bfloat16)

        @pl.when(yk != y)
        def _():
            dq_copy(yk).start()

        return carry

    lax.fori_loop(0, N_Y, key_row, 0)

    total = dq_send[y].astype(jnp.float32)
    for i in range(1, N_Y):
        peer = (y + i) % N_Y
        remote(
            dq_send.at[y], dq_recv.at[peer], q_send.at[y], q_recv.at[peer], line(i)
        ).wait_recv()
        total = total + dq_recv[peer].astype(jnp.float32)
    for h in range(GROUP_Q):
        cols = slice(h * BLOCK, (h + 1) * BLOCK)
        out_ref[:, cols] = total[:, cols].T.astype(jnp.bfloat16)

    for which, first in ((0, ROWS_Q + HD), (1, ROWS_Q)):
        total = jnp.zeros((BLOCK, HD), jnp.float32)
        for i in range(N_Z):
            peer = source_row * N_Z + i

            @pl.when(peer != me)
            def _():
                remote(
                    kv_send.at[which, 0], kv_recv.at[which, i], o_send.at[which, 0],
                    o_recv.at[which, i], peer,
                ).wait_recv()

            total = total + kv_recv[which, i].astype(jnp.float32)
        out_ref[:, first : first + HD] = total.astype(jnp.bfloat16)

    for i in range(1, N_Y):
        d_copy(i, y).wait_send()
        st_copy(i, y).wait_send()
        pt_copy(i, y).wait_send()
        dq_copy((y + i) % N_Y).wait_send()
    for which in range(2):
        for yk in range(N_Y):
            for h in range(2):

                @pl.when(yk * N_Z + 2 * pair_of(yk) + h != me)
                def _():
                    block_copy(which, yk, h).wait_send()


def attention(full_grad, q5, qt, kv, gathered):
    bf, f32 = jnp.bfloat16, jnp.float32
    vmem = pl.BlockSpec(memory_space=pltpu.VMEM)
    dma = pltpu.SemaphoreType.DMA
    units = N_Y * N_Y
    return pl.pallas_call(
        attention_kernel,
        name="attention_grads",
        out_shape=jax.ShapeDtypeStruct((BLOCK, ROWS_Q + 2 * HD), bf),
        in_specs=[vmem, vmem, vmem, vmem, pl.BlockSpec(memory_space=pl.ANY)],
        out_specs=vmem,
        scratch_shapes=[
            pltpu.VMEM((D, ROWS_Q), bf),
            pltpu.VMEM((N_Y, PAIR, HD), bf),
            pltpu.VMEM((N_Y, PAIR, HD), bf),
            pltpu.VMEM((N_Y, HD, PAIR), bf),
            pltpu.VMEM((N_Y, HD, ROWS_Q), bf),
            pltpu.VMEM((N_Y, ROWS_Q, HD), bf),
            pltpu.VMEM((units, PAIR, ROWS_Q), f32),
            pltpu.VMEM((units, PAIR, ROWS_Q), f32),
            pltpu.VMEM((PAIR, ROWS_Q), bf),
            pltpu.VMEM((PAIR, ROWS_Q), bf),
            pltpu.VMEM((N_Y, 8, ROWS_Q), f32),
            pltpu.VMEM((N_Y, 8, ROWS_Q), f32),
            pltpu.VMEM((N_Y, 8, ROWS_Q), f32),
            pltpu.VMEM((8, ROWS_Q), f32),
            pltpu.VMEM((8, ROWS_Q), f32),
            pltpu.VMEM((N_Y, 8, ROWS_Q), f32),
            pltpu.VMEM((N_Y, 8, ROWS_Q), f32),
            pltpu.VMEM((N_Y, HD, ROWS_Q), f32),
            pltpu.VMEM((N_Y, PAIR, HD), f32),
            pltpu.VMEM((N_Y, PAIR, HD), f32),
            pltpu.VMEM((N_Y, HD, ROWS_Q), bf),
            pltpu.VMEM((N_Y, HD, ROWS_Q), bf),
            pltpu.VMEM((2, 2 * N_Y, BLOCK, HD), bf),
            pltpu.VMEM((2, N_Z, BLOCK, HD), bf),
            dma,
            dma((N_Y,)), dma((N_Y,)),
            dma((N_Y,)), dma((N_Y,)),
            dma((N_Y,)), dma((N_Y,)),
            dma((N_Y,)), dma((N_Y,)),
            dma((2, 2 * N_Y)), dma((2, N_Z)),
        ],
        cost_estimate=pl.CostEstimate(
            flops=6_000_000_000, bytes_accessed=12_000_000, transcendentals=3_000_000
        ),
        compiler_params=pltpu.CompilerParams(
            collective_id=4, has_side_effects=True, vmem_limit_bytes=56 * 2**20
        ),
    )(full_grad, q5, qt, kv, gathered)


def dot_nt(a, b):
    return lax.dot_general(a, b, (((1,), (1,)), ((), ())), preferred_element_type=jnp.float32)


def expert_kernel(
    pack_ref, hidden_ref, grad_ref, q_ref, key_ref, value_ref,
    down_ref, gate_ref, up_ref, wg_ref, wu_ref, wt_ref,
    dh_ref, stat_ref, full_ref, q5_ref, qt_ref, kv_ref, all_ref,
    down, wg, wu, slots_out, recv_d, flat, slots, own, sib_out, sib_in, x_out, x_in,
    prod_buf, slope_buf, act_buf, gu, acc, back, ret, rt_out, rt_in, terms, pick, picked, stats, square, full, q5, kv_out, kv,
    w_sem, d_send, d_recv, s_send, s_recv, x_send, x_recv, ax_send, ax_recv, af_send, af_recv,
    as_send, as_recv, b_send, b_recv, t_send, t_recv, fx_send, fx_recv, fs_send, fs_recv,
    q_send, q_recv, k_send, k_recv, r_send, r_recv,
    wz_send, wz_recv, wy_send, wy_recv, wf_send, wf_recv, wo_sem,
):
    me = lax.axis_index("ctx")
    tp = lax.axis_index("tp")
    y, z = me // N_Z, me % N_Z
    x, k = tp // 2, tp % 2
    sibling = 2 * x + (1 - k)
    far = (2, 1, 3)
    near = (1, 3)
    rows_by_chunk = (y, y + 1 - 2 * (y % 2), (y + 2) % N_Y, N_Y - 1 - y)

    def chip(dx):
        return (x + dx) % N_X

    def remote(src, dst, send, recv, ctx, peer):
        return pltpu.make_async_remote_copy(
            src_ref=src, dst_ref=dst, send_sem=send, recv_sem=recv,
            device_id=(ctx, peer), device_id_type=MESH,
        )

    barrier = pltpu.get_barrier_semaphore()

    def greet_ctx(i, carry):
        pl.semaphore_signal(
            barrier, inc=1, device_id=((me + i) % N_CTX, tp), device_id_type=MESH
        )
        return carry

    def greet_tp(i, carry):
        pl.semaphore_signal(
            barrier, inc=1, device_id=(me, (tp + i) % N_TP), device_id_type=MESH
        )
        return carry

    lax.fori_loop(1, N_CTX, greet_ctx, 0)
    lax.fori_loop(1, N_TP, greet_tp, 0)

    w_copies = [
        pltpu.make_async_copy(down_ref, down, w_sem.at[0]),
        pltpu.make_async_copy(wg_ref, wg, w_sem.at[1]),
        pltpu.make_async_copy(wu_ref, wu, w_sem.at[2]),
    ]
    for copy in w_copies:
        copy.start()

    def turn(row):
        return jnp.broadcast_to(row, (BLOCK, BLOCK)).T

    ids = jnp.broadcast_to(pack_ref[0:1, :], (BLOCK, BLOCK))
    ids_t = ids.T
    sub = lax.broadcasted_iota(jnp.int32, (BLOCK, BLOCK), 0)
    lan = lax.broadcasted_iota(jnp.int32, (BLOCK, BLOCK), 1)
    before = jnp.where((ids == ids_t) & (sub < lan), 1.0, 0.0)
    slot_row = pack_ref[0:1, :] * CAP + jnp.sum(before, axis=0, keepdims=True)
    slot_ids = lax.broadcasted_iota(jnp.int32, (EXPERTS * CAP, BLOCK), 0).astype(jnp.float32)
    placing = jnp.where(slot_ids == slot_row, 1.0, 0.0).astype(jnp.bfloat16)
    placed = mm(placing, grad_ref[...])
    for e in range(EXPERTS):
        slots_out[e] = placed[e * CAP : (e + 1) * CAP].astype(jnp.bfloat16)
    for h in range(GROUP_Q):
        heads = slice(h * BLOCK, (h + 1) * BLOCK)
        q5[y, heads, :] = q_ref[:, heads]
    kv_out[0] = key_ref[...]
    kv_out[1] = value_ref[...]
    pl.semaphore_wait(barrier, N_CTX - 1 + N_TP - 1)

    def exchange(buf, x_s, x_r, f_s, f_r, s_s, s_r):
        def send_near(ch):
            rows = chunk_rows(ch)
            for i, dx in enumerate(near):
                remote(
                    buf.at[tp, rows], buf.at[tp, rows], x_s.at[i, ch], x_r.at[i, ch],
                    me, 2 * chip(dx) + k,
                ).start()
            share(tp, 3, ch).start()

        def source(i):
            return 2 * chip(N_X - near[i]) + k

        def share(t, i, ch):
            rows = chunk_rows(ch)
            return remote(
                buf.at[t, rows], buf.at[t, rows], s_s.at[i, ch], s_r.at[i, ch], me, sibling
            )

        def half(i, ch):
            start = rows_by_chunk[ch] * CHUNK + i * (CHUNK // 2)
            return pl.ds(pl.multiple_of(start, CHUNK // 2), CHUNK // 2)

        def pass_on(i, ch):
            rows = half(i, ch)
            t = source(i)
            return remote(
                buf.at[t, rows], buf.at[t, rows], f_s.at[i, ch], f_r.at[i, ch],
                me, 2 * chip(near[i]) + k,
            )

        def get_near(ch):
            rows = chunk_rows(ch)
            for i in range(2):
                t = source(i)
                remote(
                    buf.at[t, rows], buf.at[t, rows], x_s.at[i, ch], x_r.at[i, ch], me, t
                ).wait_recv()
                pass_on(i, ch).start()
                share(t, i, ch).start()

        opposite = 2 * chip(2) + k

        def get_far(ch):
            for i in range(2):
                rows = half(i, ch)
                remote(
                    buf.at[opposite, rows], buf.at[opposite, rows], f_s.at[i, ch], f_r.at[i, ch],
                    me, opposite,
                ).wait_recv()
            share(opposite, 2, ch).start()

        def shared(i):
            return (source(0), source(1), opposite, tp)[i] + 1 - 2 * k

        def get_shared(i, ch):
            share(shared(i), i, ch).wait_recv()

        def drain(ch):
            rows = chunk_rows(ch)
            for i in range(2):
                remote(
                    buf.at[tp, rows], buf.at[tp, rows], x_s.at[i, ch], x_r.at[i, ch],
                    me, 2 * chip(near[i]) + k,
                ).wait_send()
                pass_on(i, ch).wait_send()
            for i in range(4):
                share(tp, i, ch).wait_send()

        return send_near, get_near, get_far, get_shared, drain, source, opposite, shared

    def w_rows(ctx, part=None):
        if part is None:
            return pl.ds(pl.multiple_of(ctx * W_ROWS, W_ROWS), W_ROWS)
        half = W_ROWS // 2
        return pl.ds(pl.multiple_of(ctx * W_ROWS + part * half, half), half)

    def w_to(dst_rows, src, send, recv, ctx):
        return remote(src, all_ref.at[dst_rows], send, recv, ctx, tp)

    def turn_z(i, n):
        return (z + (n if i == 0 else N_Z - n)) % N_Z

    def wz(i, n):
        block = y * N_Z + turn_z(i, N_Z - n + 1)
        rows = w_rows(block, i if n == N_Z // 2 else None)
        src = wt_ref if n == 1 else all_ref.at[rows]
        return w_to(rows, src, wz_send.at[i, n - 1], wz_recv.at[i, n - 1], y * N_Z + turn_z(i, 1))

    def wz_wait(i, n):
        rows = w_rows(y * N_Z + turn_z(i, N_Z - n), i if n == N_Z // 2 else None)
        w_to(
            rows, all_ref.at[rows], wz_send.at[i, n - 1], wz_recv.at[i, n - 1],
            y * N_Z + turn_z(1 - i, 1),
        ).wait_recv()

    row_order = (0, 7, 1, 6, 2, 5, 3, 4)

    def next_row(i, n=1):
        return (y + (n if i == 0 else N_Y - n)) % N_Y

    def wy(i, o):
        rows = w_rows(y * N_Z + (z + row_order[o]) % N_Z)
        src = wt_ref if o == 0 else all_ref.at[rows]
        return w_to(rows, src, wy_send.at[i, o], wy_recv.at[i, o], next_row(i) * N_Z + z)

    def wf(i, o):
        rows = w_rows(next_row(1 - i) * N_Z + (z + row_order[o]) % N_Z, i)
        return w_to(
            rows, all_ref.at[rows], wf_send.at[i, o], wf_recv.at[i, o], next_row(i) * N_Z + z
        )

    w_own = pltpu.make_async_copy(wt_ref, all_ref.at[w_rows(me)], wo_sem)

    def ring_first():
        w_own.start()
        for i in range(2):
            wz(i, 1).start()
            wy(i, 0).start()

    def ring_step(n):
        for i in range(2):
            wz_wait(i, n)
        if n < N_Z // 2:
            for i in range(2):
                wz(i, n + 1).start()
        for o in (2 * n - 1, 2 * n) if n < N_Z // 2 else (N_Z - 1,):
            for i in range(2):
                wy(i, o).start()

    def row_step(o):
        for i in range(2):
            rows = w_rows(next_row(1 - i) * N_Z + (z + row_order[o]) % N_Z)
            w_to(
                rows, all_ref.at[rows], wy_send.at[i, o], wy_recv.at[i, o],
                next_row(1 - i) * N_Z + z,
            ).wait_recv()
            wf(i, o).start()

    def ring_last():
        w_own.wait()
        for o in range(N_Z):
            for i in range(2):
                rows = w_rows(next_row(i, 2) * N_Z + (z + row_order[o]) % N_Z, i)
                w_to(
                    rows, all_ref.at[rows], wf_send.at[i, o], wf_recv.at[i, o],
                    next_row(1 - i) * N_Z + z,
                ).wait_recv()

    def ring_drain():
        for i in range(2):
            for n in range(1, N_Z // 2 + 1):
                wz(i, n).wait_send()
            for o in range(N_Z):
                wy(i, o).wait_send()
                wf(i, o).wait_send()

    def chunk_rows(ch):
        return pl.ds(pl.multiple_of(rows_by_chunk[ch] * CHUNK, CHUNK), CHUNK)

    def pair_first(p):
        return 2 * (y // 2) if p == 0 else 2 - 2 * (y // 2)

    def pair_rows(p):
        return pl.ds(pl.multiple_of(pair_first(p) * CHUNK, PAIR_ROWS), PAIR_ROWS)

    hid_x = exchange(gu, ax_send, ax_recv, af_send, af_recv, as_send, as_recv)
    source, opposite, shared = hid_x[5:]

    def dispatch(j):
        return remote(
            slots_out.at[j // GROUP], recv_d.at[me], d_send.at[j], d_recv.at[me], j, tp
        )

    def dispatch_row(ch):
        row = rows_by_chunk[ch]

        def send_step(dz, carry):
            dispatch(row * N_Z + (z + dz) % N_Z).start()
            return carry

        lax.fori_loop(1 if ch == 0 else 0, N_Z, send_step, 0)

    recv_d[me] = slots_out[me // GROUP]

    def q_copy(i, owner):
        ctx = ((y + i) % N_Y) * N_Z + z
        return remote(q5.at[owner], q5.at[owner], q_send.at[i], q_recv.at[owner], ctx, tp)

    def turn_queries():
        for i in range(1, N_Y):
            q_copy(i, (y + i) % N_Y).wait_recv()
        q5_ref[...] = q5[...]
        for r in range(N_Y):
            for h in range(GROUP_Q):
                heads = slice(h * BLOCK, (h + 1) * BLOCK)
                qt_ref[r, :, heads] = q5[r, heads, :].astype(jnp.float32).T.astype(jnp.bfloat16)

    user_row = (y - z // 2 + N_Y) % N_Y

    def kv_copy(i):
        return remote(
            kv_out, kv.at[y, z % 2], k_send.at[i], k_recv.at[y, z % 2], user_row * N_Z + i, tp
        )

    def send_keys():
        for i in range(N_Z):

            @pl.when(user_row * N_Z + i != me)
            def _():
                kv_copy(i).start()

        @pl.when(user_row == y)
        def _():
            kv[y, z % 2] = kv_out[...]

    def get_keys():
        for r in range(N_Y):
            for h in range(2):
                peer = r * N_Z + 2 * ((r - y + N_Y) % N_Y) + h

                @pl.when(peer != me)
                def _():
                    remote(
                        kv_out, kv.at[r, h], k_send.at[0], k_recv.at[r, h], peer, tp
                    ).wait_recv()

        kv_ref[...] = kv[...]

    def arrive(ch):
        first = rows_by_chunk[ch] * N_Z
        for i in range(N_Z):
            j = first + i

            @pl.when(j != me)
            def _():
                remote(
                    slots_out.at[0], recv_d.at[j], d_send.at[j], d_recv.at[j], j, tp
                ).wait_recv()

            flat[i * CAP : (i + 1) * CAP, :] = recv_d[j].astype(jnp.float32)
        slots[chunk_rows(ch), :] = flat[...].astype(jnp.bfloat16)

    def sib_copy(i, ch):
        rows = chunk_rows(ch)
        return remote(
            sib_out.at[i, rows], sib_in.at[i, rows], s_send.at[i, ch], s_recv.at[i, ch],
            me, sibling,
        )

    def x_copy(i, ch):
        rows = chunk_rows(ch)
        return remote(
            x_out.at[i, rows], x_in.at[i, rows], x_send.at[i, ch], x_recv.at[i, ch],
            me, 2 * chip(far[i]) + k,
        )

    def stage1(ch):
        rows = chunk_rows(ch)
        part = slots[rows, :]
        for i, dx in enumerate(far + (0,)):
            base = 2 * chip(dx)

            def block(t):
                start = pl.multiple_of(t * FF_DEV, FF_DEV)
                return dot_nt(part, down[pl.ds(start, FF_DEV), :]).astype(jnp.bfloat16)

            sib_out[i, rows, :] = block(base + 1 - k)
            sib_copy(i, ch).start()
            own[i, rows, :] = block(base + k)

    def joined(i, ch):
        rows = chunk_rows(ch)
        sib_copy(i, ch).wait_recv()
        return own[i, rows, :].astype(jnp.float32) + sib_in[i, rows, :].astype(jnp.float32)

    def stage2(ch):
        rows = chunk_rows(ch)
        for i in range(3):
            x_out[i, rows, :] = joined(i, ch).astype(jnp.bfloat16)
            x_copy(i, ch).start()

    def rt_copy(j, ch):
        return remote(rt_out.at[ch], rt_in.at[me], r_send.at[j], r_recv.at[me], j, tp)

    def stage3(ch):
        rows = chunk_rows(ch)
        total = joined(3, ch)
        for i in range(3):
            x_copy(i, ch).wait_recv()
            total = total + x_in[i, rows, :].astype(jnp.float32)
        gu[tp, rows, 0:FF_DEV] = (total * slope_buf[rows, :]).astype(jnp.bfloat16)
        gu[tp, rows, FF_DEV : 2 * FF_DEV] = (total * act_buf[rows, :]).astype(jnp.bfloat16)
        hid_x[0](ch)
        term = jnp.sum(total * prod_buf[rows, :], axis=1, keepdims=True)
        rt_out[ch] = mm(owner_is, (term * spot_is).astype(jnp.bfloat16))
        for i in range(N_Z):
            j = rows_by_chunk[ch] * N_Z + i

            @pl.when(j != me)
            def _():
                rt_copy(j, ch).start()

        if ch == 0:
            rt_in[me] = rt_out[0]

    def product(t, p):
        rows = pair_rows(p)
        cols = pl.ds(pl.multiple_of(t * FF_DEV, FF_DEV), FF_DEV)
        return dot_nt(gu[t, rows, 0:FF_DEV], wg[:, cols]) + dot_nt(
            gu[t, rows, FF_DEV : 2 * FF_DEV], wu[:, cols]
        )

    def back_copy(j):
        return remote(back.at[j], ret.at[me], b_send.at[j], b_recv.at[me], j, tp)

    def near_products(p):
        acc[p] = product(tp, p)
        for i in range(2):
            acc[p] += product(source(i), p)

    def far_products(p):
        acc[p] += product(opposite, p)
        for i in (3, 0, 1, 2):
            for ch in (2 * p, 2 * p + 1):
                hid_x[3](i, ch)
            acc[p] += product(shared(i), p)

    def give_back(p):
        for i in range(2 * N_Z):
            j = pair_first(p) * N_Z + i
            back[j] = acc[p, i * CAP : (i + 1) * CAP, :].astype(jnp.bfloat16)

            @pl.when(j != me)
            def _():
                back_copy(j).start()

    for ch in range(N_Y):
        dispatch_row(ch)
    gate = gate_ref[...].astype(jnp.float32).T
    up = up_ref[...].astype(jnp.float32).T
    act, slope = silu_parts(gate)
    slope_buf[...] = up * slope
    act_buf[...] = act
    prod_buf[...] = act * up
    ring_first()
    slot_col = turn(slot_row)[:, 0:1]
    number = lax.broadcasted_iota(jnp.int32, (8, N_Y * N_Z * CAP_PAD), 1).astype(jnp.float32)
    device_row = jnp.floor((number + 0.5) / (N_Z * CAP_PAD))
    within = number - device_row * (N_Z * CAP_PAD)
    device = jnp.floor((within + 0.5) / CAP)
    column = (
        jnp.floor((device_row * N_Z + device + 0.5) / GROUP) * CAP + within - device * CAP
    )
    column = jnp.where(within < CHUNK, column, -1.0)
    pick[...] = jnp.where(column[0:1, :] == slot_col, 1.0, 0.0).astype(jnp.bfloat16)
    score = turn(pack_ref[1:2, :])[:, 0:1]
    gain_val = jnp.concatenate([pack_ref[2 + h : 3 + h, :] for h in range(GROUP_Q)], axis=1)

    spot = lax.broadcasted_iota(jnp.int32, (CHUNK, BLOCK), 0).astype(jnp.float32)
    spot = spot - CAP * jnp.floor((spot + 0.5) / CAP)
    spot_is = jnp.where(
        spot == lax.broadcasted_iota(jnp.int32, (CHUNK, BLOCK), 1).astype(jnp.float32), 1.0, 0.0
    )
    own_sub = lax.broadcasted_iota(jnp.int32, (N_Z, CHUNK), 0) * CAP
    own_lan = lax.broadcasted_iota(jnp.int32, (N_Z, CHUNK), 1)
    owner_is = jnp.where((own_lan >= own_sub) & (own_lan < own_sub + CAP), 1.0, 0.0)
    owner_is = owner_is.astype(jnp.bfloat16)
    hidden_val = hidden_ref[...].astype(jnp.float32)
    square[...] = jnp.broadcast_to(
        jnp.sum(hidden_val * hidden_val, axis=1, keepdims=True), square.shape
    )
    w_copies[0].wait()
    arrive(0)
    stage1(0)
    arrive(1)
    stage1(1)
    stage2(0)
    arrive(2)
    stage1(2)
    stage2(1)
    arrive(3)
    stage1(3)
    stage2(2)
    stage2(3)
    send_keys()
    for i in range(1, N_Y):
        q_copy(i, y).start()
    ring_step(1)
    row_step(0)
    stage3(0)
    ring_step(2)
    stage3(1)
    row_step(1)
    row_step(2)
    stage3(2)
    stage3(3)
    ring_step(3)
    turn_queries()
    w_copies[1].wait()
    w_copies[2].wait()
    hid_x[1](0)
    hid_x[1](1)
    near_products(0)
    hid_x[1](2)
    hid_x[1](3)
    hid_x[2](0)
    hid_x[2](1)
    ring_step(4)
    far_products(0)
    give_back(0)
    near_products(1)
    row_step(3)
    hid_x[2](2)
    hid_x[2](3)
    far_products(1)
    give_back(1)
    row_step(4)
    row_step(5)
    row_step(6)
    ret[me] = back[me]
    row_step(7)
    get_keys()

    for j in range(N_CTX):

        @pl.when(j != me)
        def _():
            remote(rt_out.at[0], rt_in.at[j], r_send.at[j], r_recv.at[j], j, tp).wait_recv()

        terms[j : j + 1, :] = rt_in[j, pl.ds(z, 1), :]
    expert_col = turn(pack_ref[0:1, :])[:, 0:1]
    rank_col = slot_col - CAP * expert_col
    member = lax.broadcasted_iota(jnp.int32, (BLOCK, N_CTX), 1)
    member = jnp.floor((member.astype(jnp.float32) + 0.5) / GROUP)
    member_is = jnp.where(member == expert_col, 1.0, 0.0).astype(jnp.bfloat16)
    token_terms = mm(member_is, terms[...].astype(jnp.bfloat16))
    router_tok = jnp.sum(
        jnp.where(lan.astype(jnp.float32) == rank_col, token_terms, 0.0), axis=1, keepdims=True
    )
    picked[...] = jnp.zeros_like(picked)
    for ch in range(N_Y):
        first = rows_by_chunk[ch] * N_Z
        for i in range(N_Z):
            j = first + i

            @pl.when(j != me)
            def _():
                remote(back.at[j], ret.at[j], b_send.at[j], b_recv.at[j], j, tp).wait_recv()

            flat[i * CAP : (i + 1) * CAP, :] = ret[j].astype(jnp.float32)
        cols = pl.ds(pl.multiple_of(first * CAP_PAD, N_Z * CAP_PAD), N_Z * CAP_PAD)
        picked[...] += mm(pick[:, cols][:, 0:CHUNK], flat[...].astype(jnp.bfloat16))

    norm_grad = picked[...] * score
    hidden_now = hidden_ref[...].astype(jnp.float32)
    cross = jnp.sum(hidden_now * gain_val * norm_grad, axis=1, keepdims=True)
    packed = jnp.where(
        lan == 0, router_tok, jnp.where(lan == 1, square[...], cross)
    )
    stats[tp] = packed.T[0:8, :]

    def stat_copy(peer, src):
        return remote(
            stats.at[src], stats.at[src], t_send.at[peer], t_recv.at[src], me, peer
        )

    def stat_start(i, carry):
        stat_copy((tp + i) % N_TP, tp).start()
        return carry

    def stat_wait(i, carry):
        stat_copy((tp + i) % N_TP, (tp + i) % N_TP).wait_recv()
        return carry

    lax.fori_loop(1, N_TP, stat_start, 0)
    lax.fori_loop(1, N_TP, stat_wait, 0)
    total = stats[0]
    for t in range(1, N_TP):
        total = total + stats[t]
    stat_ref[...] = total
    spread = jnp.concatenate([total] * (BLOCK // 8), axis=0).T
    inverse_rms = lax.rsqrt(spread[:, 1:2] / D + EPSILON)
    cross_sum = spread[:, 2:3]
    d_hidden = (
        grad_ref[...].astype(jnp.float32)
        + inverse_rms * gain_val * norm_grad
        - hidden_now * inverse_rms * inverse_rms * inverse_rms * cross_sum / D
    ).astype(jnp.bfloat16)
    dh_ref[...] = d_hidden
    full[tp] = d_hidden

    def full_chip(i):
        return 2 * chip(N_X - far[i]) + k

    def full_out(i):
        return remote(
            full.at[tp], full.at[tp], fx_send.at[i], fx_recv.at[i], me, 2 * chip(far[i]) + k
        )

    def full_share(t, i):
        return remote(full.at[t], full.at[t], fs_send.at[i], fs_recv.at[i], me, sibling)

    for i in range(3):
        full_out(i).start()
    full_share(tp, 3).start()
    for i in (1, 2, 0):
        t = full_chip(i)
        remote(full.at[t], full.at[t], fx_send.at[i], fx_recv.at[i], me, t).wait_recv()
        full_share(t, i).start()
    for i in (3, 1, 2, 0):
        t = sibling if i == 3 else full_chip(i) + 1 - 2 * k
        full_share(t, i).wait_recv()
    full_ref[...] = full[...]
    ring_last()

    ring_drain()
    def drain_ctx(i, carry):
        j = (me + i) % N_CTX
        dispatch(j).wait_send()
        back_copy(j).wait_send()
        rt_copy(j, 0).wait_send()
        return carry

    def drain_tp(i, carry):
        stat_copy((tp + i) % N_TP, tp).wait_send()
        return carry

    lax.fori_loop(1, N_CTX, drain_ctx, 0)
    lax.fori_loop(1, N_TP, drain_tp, 0)
    for ch in range(N_Y):
        for i in range(4):
            sib_copy(i, ch).wait_send()
        for i in range(3):
            x_copy(i, ch).wait_send()
        hid_x[4](ch)
    for i in range(1, N_Y):
        q_copy(i, y).wait_send()
    for i in range(N_Z):

        @pl.when(user_row * N_Z + i != me)
        def _():
            kv_copy(i).wait_send()

    for i in range(3):
        full_out(i).wait_send()
    for i in range(4):
        full_share(tp, i).wait_send()


def expert_block(pack, hidden, grad, queries, keys, values, down, gate, up, wg, wu, w_out_t):
    bf, f32 = jnp.bfloat16, jnp.float32
    vmem = pl.BlockSpec(memory_space=pltpu.VMEM)
    hbm = pl.BlockSpec(memory_space=pl.ANY)
    dma = pltpu.SemaphoreType.DMA
    return pl.pallas_call(
        expert_kernel,
        name="expert_block",
        out_shape=[
            jax.ShapeDtypeStruct((BLOCK, FEAT), bf),
            jax.ShapeDtypeStruct((8, BLOCK), f32),
            jax.ShapeDtypeStruct((N_TP, BLOCK, FEAT), bf),
            jax.ShapeDtypeStruct((N_Y, ROWS_Q, HD), bf),
            jax.ShapeDtypeStruct((N_Y, HD, ROWS_Q), bf),
            jax.ShapeDtypeStruct((N_Y, 2, 2, BLOCK, HD), bf),
            jax.ShapeDtypeStruct((D, ROWS_Q), bf),
        ],
        in_specs=[vmem] * 6 + [hbm, vmem, vmem, hbm, hbm, hbm],
        out_specs=[vmem] * 6 + [hbm],
        scratch_shapes=[
            pltpu.VMEM((FF_GRP, FEAT), bf),
            pltpu.VMEM((FEAT, FF_GRP), bf),
            pltpu.VMEM((FEAT, FF_GRP), bf),
            pltpu.VMEM((EXPERTS, CAP, FEAT), bf),
            pltpu.VMEM((N_CTX, CAP, FEAT), bf),
            pltpu.VMEM((CHUNK, FEAT), f32),
            pltpu.VMEM((SLOTS, FEAT), bf),
            pltpu.VMEM((4, SLOTS, FF_DEV), bf),
            pltpu.VMEM((4, SLOTS, FF_DEV), bf),
            pltpu.VMEM((4, SLOTS, FF_DEV), bf),
            pltpu.VMEM((3, SLOTS, FF_DEV), bf),
            pltpu.VMEM((3, SLOTS, FF_DEV), bf),
            pltpu.VMEM((SLOTS, FF_DEV), f32),
            pltpu.VMEM((SLOTS, FF_DEV), f32),
            pltpu.VMEM((SLOTS, FF_DEV), f32),
            pltpu.VMEM((N_TP, SLOTS, 2 * FF_DEV), bf),
            pltpu.VMEM((2, PAIR_ROWS, FEAT), f32),
            pltpu.VMEM((N_CTX, CAP, FEAT), bf),
            pltpu.VMEM((N_CTX, CAP, FEAT), bf),
            pltpu.VMEM((N_Y, N_Z, BLOCK), f32),
            pltpu.VMEM((N_CTX, N_Z, BLOCK), f32),
            pltpu.VMEM((N_CTX, BLOCK), f32),
            pltpu.VMEM((BLOCK, N_Y * N_Z * CAP_PAD), bf),
            pltpu.VMEM((BLOCK, FEAT), f32),
            pltpu.VMEM((N_TP, 8, BLOCK), f32),
            pltpu.VMEM((BLOCK, HD), f32),
            pltpu.VMEM((N_TP, BLOCK, FEAT), bf),
            pltpu.VMEM((N_Y, ROWS_Q, HD), bf),
            pltpu.VMEM((2, BLOCK, HD), bf),
            pltpu.VMEM((N_Y, 2, 2, BLOCK, HD), bf),
            dma((3,)),
            dma((N_CTX,)), dma((N_CTX,)),
            dma((4, N_Y)), dma((4, N_Y)),
            dma((3, N_Y)), dma((3, N_Y)),
            dma((2, N_Y)), dma((2, N_Y)),
            dma((2, N_Y)), dma((2, N_Y)),
            dma((4, N_Y)), dma((4, N_Y)),
            dma((N_CTX,)), dma((N_CTX,)),
            dma((N_TP,)), dma((N_TP,)),
            dma((3,)), dma((3,)),
            dma((4,)), dma((4,)),
            dma((N_Y,)), dma((N_Y,)),
            dma((N_Z,)), dma((N_Y, 2)),
            dma((N_CTX,)), dma((N_CTX,)),
            dma((2, N_Z // 2)), dma((2, N_Z // 2)),
            dma((2, N_Z)), dma((2, N_Z)),
            dma((2, N_Z)), dma((2, N_Z)),
            dma,
        ],
        cost_estimate=pl.CostEstimate(
            flops=60_000_000_000, bytes_accessed=200_000_000, transcendentals=3_000_000
        ),
        compiler_params=pltpu.CompilerParams(
            collective_id=3, has_side_effects=True, vmem_limit_bytes=56 * 2**20
        ),
    )(pack, hidden, grad, queries, keys, values, down, gate, up, wg, wu, w_out_t)


def body(
    hidden_in,
    norm_gain,
    out_grad,
    router_score,
    expert_ids,
    gate_saved,
    up_saved,
    w_gate,
    w_up,
    w_down,
    w_out,
    queries,
    keys,
    values,
):
    pack = jnp.concatenate(
        [
            expert_ids.reshape(1, BLOCK).astype(jnp.float32),
            router_score.astype(jnp.float32).reshape(1, BLOCK),
            norm_gain.astype(jnp.float32).reshape(GROUP_Q, BLOCK),
            jnp.zeros((1, BLOCK), jnp.float32),
        ],
        axis=0,
    )
    d_hidden, stats, full_grad, q5, qt, kv, gathered = expert_block(
        pack,
        hidden_in,
        out_grad,
        queries,
        keys,
        values,
        w_down[0],
        gate_saved[0],
        up_saved[0],
        w_gate[0],
        w_up[0],
        w_out.T,
    )
    router_grad = stats[0]
    grads = attention(full_grad, q5, qt, kv, gathered)
    query_grad = grads[:, 0:ROWS_Q]
    key_grad = grads[:, ROWS_Q : ROWS_Q + HD]
    value_grad = grads[:, ROWS_Q + HD :]
    return (
        d_hidden,
        router_grad,
        query_grad,
        key_grad,
        value_grad,
    )


def solution(mesh):
    in_specs = (
        P("ctx", "tp"),
        P("tp"),
        P("ctx", "tp"),
        P("ctx"),
        P("ctx", None),
        P("ctx", "tp", None),
        P("ctx", "tp", None),
        P("ctx", "tp", None),
        P("ctx", "tp", None),
        P("ctx", None, "tp"),
        P("tp", "ctx"),
        P("ctx", "tp"),
        P("ctx", "tp"),
        P("ctx", "tp"),
    )
    out_specs = (P("ctx", "tp"), P("ctx"), P("ctx", "tp"), P("ctx", "tp"), P("ctx", "tp"))
    return jax.shard_map(body, mesh=mesh, in_specs=in_specs, out_specs=out_specs, check_vma=False)
```
